512 devices in a mesh: panel: 64 (over x, z), obs: 8 (over y, core).
Axes of the slice: x: 4, y: 4, z: 16, core: 2. Of those that a mesh axis runs over, the one named last changes fastest.
Arguments:
- donor: bfloat16 [512, 125, 4, 1024], P('panel', None, None, 'obs'), may hold values from -6 to 6
- donor_elem: int32 [8192], P('obs'), may hold values from 0 to 1023, as said below
- local_coords: float32 [3, 8192], P(None, 'obs'), may hold values from -1 to 1
- owner: int32 [8192], replicated, may hold values from 0 to 63, as said below
- weights: bfloat16 [1024, 4, 4, 8192], P('obs', None, None, 'panel'), may hold values from -0.015625 to 0.015625
- offsets: int32 [8, 64], P('obs', 'panel'), may hold values from 0 to 256
Outputs:
- pressure: float32 [512, 1024], P('panel', 'obs')
The draws below stay inside these ranges and needn't reach their ends.
Inputs may be any that keep to these rules, and one draw needn't show every extreme that they name: `donor_elem`: point i lies in a donor element of the i // 1024-th block of 128 elements. Every owner owns exactly 128 points. Within each of the 8 aligned blocks of 1024 points an owner appears either 44 times or 128 / 8 - 128 / 32 times, and exactly one block holds 44 of its points.
All inputs are finite; a program needn't handle non-finite values.
Results may differ from the reference program's by a relative error of at most 0.0029.
Values may be sent and summed in bfloat16 or wider, within the bound.
A program may use at most 64 MiB of HBM per device.

```python
import jax
import jax.numpy as jnp
from jax import lax

PS = 128
ELEMS_DEV = 128
QUANT = 4
NODES = 125
BAND = 4
OBLK = 128
PTILE = 128
TW = 512
MAXOFF = 256
P_ALL = 8192
ELEMS = 1024
OBSERVERS = 1024
N_PANEL = 64
N_OBS = 8


def draw_donor_elem(key, part):
    share_size = P_ALL // N_OBS
    picks = jax.random.randint(key, (P_ALL,), 0, ELEMS_DEV)
    share_ids = jnp.arange(P_ALL, dtype=jnp.int32) // share_size
    return (share_ids * ELEMS_DEV + picks).astype(jnp.int32)


def shuffle_row(row_key, row_values):
    return row_values[jax.random.permutation(row_key, row_values.shape[0])]


def draw_owner(key, part):
    share_size = P_ALL // N_OBS
    mean_count = PS // N_OBS
    lift = mean_count // 4
    key_shift = jax.random.fold_in(key, 11)
    key_order = jax.random.fold_in(key, 23)
    rotation = jax.random.permutation(key_shift, N_PANEL) % N_OBS
    share_ids = jnp.arange(N_OBS, dtype=jnp.int32)
    phase = (share_ids[:, None] + rotation[None, :]) % N_OBS
    counts = jnp.where(phase == 0, mean_count + (N_OBS - 1) * lift, mean_count - lift)
    bounds = jnp.cumsum(counts, axis=1)
    slot_ids = jnp.arange(share_size, dtype=jnp.int32)
    sorted_owner = jnp.sum((bounds[:, None, :] <= slot_ids[None, :, None]).astype(jnp.int32), axis=2)
    row_keys = jax.random.split(key_order, N_OBS)
    mixed = jax.vmap(shuffle_row)(row_keys, sorted_owner)
    return mixed.reshape(-1).astype(jnp.int32)


def draw_offsets(key, part):
    block_rows = OBSERVERS // OBLK
    tile_cols = P_ALL // PTILE
    key_values = jax.random.fold_in(key, 5)
    key_spots = jax.random.fold_in(key, 7)
    values = jax.random.randint(key_values, (block_rows * tile_cols,), 0, MAXOFF + 1)
    spots = jax.random.permutation(key_spots, block_rows * tile_cols)
    values = values.at[spots[0]].set(MAXOFF)
    values = values.at[spots[1]].set(0)
    return values.reshape(block_rows, tile_cols).astype(jnp.int32)


def shard_levels(stream_key, shape, shards, least, high):
    gain = 1.0
    for axis_at, parts in shards:
        draws = jax.random.uniform(jax.random.fold_in(jax.random.fold_in(stream_key, 6), axis_at), (parts,), jnp.float32, least / len(shards), high / len(shards))
        gain = gain * jnp.repeat(jnp.exp(draws), shape[axis_at] // parts).reshape((-1,) + (1,) * (len(shape) - 1 - axis_at))
    return gain


def scatter_about(stream_key, shape, spread, most, cuts=(), kind=jnp.bfloat16):
    result = spread * jax.random.normal(stream_key, shape, jnp.float32)
    if cuts:
        result = result * shard_levels(stream_key, shape, cuts, -0.22, 0.18)
    return jnp.clip(result, -most, most).astype(kind)


def setup_inputs(seed: int = 0) -> dict:
    key_list = jax.random.split(jax.random.key(seed), 7)
    donor = scatter_about(key_list[0], (TW, NODES, QUANT, ELEMS), 1.0, 6.0, ((0, 64), (3, 8)))
    donor_elem = draw_donor_elem(jax.random.fold_in(key_list[6], 71), 0)
    local_coords = jnp.clip(jax.random.uniform(key_list[2], (3, P_ALL), jnp.float32, -1.0, 1.0) * shard_levels(key_list[2], (3, P_ALL), ((1, 8),), -0.4, 0.0), -1.0, 1.0)
    owner = draw_owner(jax.random.fold_in(key_list[6], 71), 0)
    weights = scatter_about(key_list[4], (OBSERVERS, BAND, QUANT, P_ALL), (P_ALL * QUANT * BAND) ** -0.5, 0.015625, ((0, 8), (3, 64)))
    offsets = draw_offsets(jax.random.fold_in(key_list[6], 71), 0)
    return {"donor": donor, "donor_elem": donor_elem, "local_coords": local_coords, "owner": owner, "weights": weights, "offsets": offsets}


NODE_SPOTS = (-1.0, -0.5, 0.0, 0.5, 1.0)


def lagrange_table(coords):
    factors = []
    for direction in range(3):
        coord_row = coords[direction]
        columns = []
        for node_one in range(5):
            weighting = jnp.ones_like(coord_row)
            for node_two in range(5):
                if node_two != node_one:
                    weighting = weighting * ((coord_row - NODE_SPOTS[node_two]) / (NODE_SPOTS[node_one] - NODE_SPOTS[node_two]))
            columns.append(weighting)
        factors.append(jnp.stack(columns))
    node_table = factors[0][:, None, None, :] * factors[1][None, :, None, :] * factors[2][None, None, :, :]
    return node_table.reshape(125, coords.shape[1])


def reference(donor, donor_elem, local_coords, owner, weights, offsets):
    node_table = lagrange_table(local_coords)

    def one_time(moment):
        values = jnp.take(moment, donor_elem, axis=2).astype(jnp.float32)
        return jnp.sum(node_table[:, None, :] * values, axis=0).astype(jnp.bfloat16)

    sources = lax.map(one_time, donor)
    order = jnp.argsort(owner, stable=True).astype(jnp.int32)
    ordered = jnp.take(sources, order, axis=2)
    padded = jnp.pad(ordered, ((BAND - 1, 0), (0, 0), (0, 0)))
    time_ids = jnp.arange(TW, dtype=jnp.int32)

    def tile_step(running, tile_id):
        start = (tile_id * PTILE).astype(jnp.int32)
        panel_piece = lax.dynamic_slice_in_dim(padded, start, PTILE, 2)
        stacked = jnp.stack([panel_piece[BAND - 1 - delay:BAND - 1 - delay + TW] for delay in range(BAND)], axis=1)
        flat = stacked.reshape(TW, BAND * QUANT * PTILE).astype(jnp.float32)
        weight_tile = lax.dynamic_slice_in_dim(weights, start, PTILE, 3).reshape(OBSERVERS, BAND * QUANT * PTILE).astype(jnp.float32)
        product = jnp.dot(flat, weight_tile.T, precision=lax.Precision.HIGHEST)
        delays = lax.dynamic_slice_in_dim(offsets, tile_id, 1, 1)[:, 0]
        delay_obs = jnp.repeat(delays, OBLK)
        source_time = time_ids[:, None] - delay_obs[None, :]
        moved = jnp.take_along_axis(product, jnp.clip(source_time, 0, TW - 1), axis=0)
        moved = jnp.where(source_time >= 0, moved, jnp.float32(0.0))
        return running + moved, None

    start_total = jnp.zeros((TW, OBSERVERS), jnp.float32)
    pressure, unused = lax.scan(tile_step, start_total, jnp.arange(P_ALL // PTILE, dtype=jnp.int32))
    return pressure
```

```python
import functools

import jax
import jax.numpy as jnp
from jax import lax
from jax.experimental import pallas as pl
from jax.experimental.pallas import tpu as pltpu
from jax.sharding import PartitionSpec as P

F32 = jnp.float32
BF16 = jnp.bfloat16
I32 = jnp.int32
SPOTS = (-1.0, -0.5, 0.0, 0.5, 1.0)
NX = 4
NZ = 16
NB = 8
FRONT = 264
TW = 512
NT = (((1,), (1,)), ((), ()))
NN = (((1,), (0,)), ((), ()))


def iota(shape, axis):
    return lax.broadcasted_iota(I32, shape, axis)


def dot(a, b, dims):
    return lax.dot_general(a, b, dims, preferred_element_type=F32)


def hit(cond):
    return jnp.where(cond, 1.0, 0.0).astype(BF16)


def pick_kernel(donor_ref, elem_ref, coord_ref, owner_ref, w_ref, base_ref, ex_ref, w2_ref,
                table, hot, src, wf):
    block = lax.axis_index("obs")
    panel = lax.axis_index("panel")

    def table_step(tile, carry):
        lanes = pl.ds(pl.multiple_of(tile * 128, 128), 128)
        factors = []
        for direction in range(3):
            x = jnp.broadcast_to(coord_ref[direction:direction + 1, lanes], (8, 128))
            column = []
            for one in range(5):
                value = None
                for two in range(5):
                    if two != one:
                        term = (x - SPOTS[two]) * (1.0 / (SPOTS[one] - SPOTS[two]))
                        value = term if value is None else value * term
                column.append(value)
            factors.append(column)
        low = iota((8, 128), 0) < 4
        pairs = [[fa * fb for fb in factors[1]] for fa in factors[0]]
        node = lambda n: pairs[n // 25][(n // 5) % 5] * factors[2][n % 5]
        nodes = [node(n) for n in range(125)]
        for j in range(125):
            table[8 * j:8 * j + 8, lanes] = jnp.where(low, nodes[(2 * j) % 125], nodes[(2 * j + 1) % 125])
        return carry

    lax.fori_loop(0, 8, table_step, 0)

    hot[...] = hit(iota((128, 1024), 0) == elem_ref[...] - block * 128)

    def point_step(tile, carry):
        lanes = pl.ds(pl.multiple_of(tile * 256, 256), 256)
        for part in range(2):
            picked = dot(donor_ref[part * 2000:part * 2000 + 2000, :], hot[:, lanes], NN)
            for half in range(2):
                prod = picked[half * 1000:half * 1000 + 1000] * table[:, lanes]
                prod = prod.reshape(125, 8, 256)
                first = jnp.sum(prod[:62], axis=0)
                last = jnp.sum(prod[63:], axis=0)
                mid = prod[62]
                step = 2 * part + half
                even = first[:4] + first[4:] + mid[:4]
                odd = last[:4] + last[4:] + mid[4:]
                for side in range(2):
                    cols = slice(side * 128, side * 128 + 128)
                    src[2 * tile + side, pl.ds(step, 4, stride=4), :] = even[:, cols]
                    src[2 * tile + side, pl.ds(16 + step, 4, stride=4), :] = odd[:, cols]
        return carry

    lax.fori_loop(0, 4, point_step, 0)
    sources = jnp.concatenate([src[tile] for tile in range(8)], axis=1).astype(BF16).astype(F32)

    own = owner_ref[pl.ds(block, 1), :]
    member = iota((64, 1024), 0) == own
    member_f = jnp.where(member, 1.0, 0.0)
    member_b = member_f.astype(BF16)
    upper = hit(iota((128, 128), 0) < iota((128, 128), 1))
    ones = jnp.ones((128, 128), BF16)
    carry = jnp.zeros((64, 128), F32)
    ranks = []
    for tile in range(8):
        cols = slice(tile * 128, tile * 128 + 128)
        below = dot(member_b[:, cols], upper, NN) + carry
        ranks.append(jnp.sum(member_f[:, cols] * below, axis=0, keepdims=True))
        carry = carry + dot(member_b[:, cols], ones, NN)
    rank = jnp.concatenate(ranks, axis=1).astype(I32)

    spot = jnp.where(rank < 12, (own & 7) * 16 + rank, -1)
    place = hit(iota((128, 1024), 0) == spot)
    group = own >> 3
    left = jnp.concatenate([jnp.where(group == g, sources, 0.0).astype(BF16) for g in range(8)], axis=0)
    grouped = dot(left, place, NT)
    row = iota((32, 128), 0)
    lane = iota((32, 128), 1)
    for g in range(8):
        x = grouped[g * 32:g * 32 + 32]
        for k in range(3):
            r, l = 4 << k, 16 << k
            rbit, lbit = (row // r) & 1, (lane // l) & 1
            up = pltpu.roll(pltpu.roll(x, 32 - r, 0), l, 1)
            down = pltpu.roll(pltpu.roll(x, r, 0), 128 - l, 1)
            x = jnp.where(rbit == lbit, x, jnp.where(rbit == 0, up, down))
        base_ref[g * 32:g * 32 + 32, :] = x.astype(BF16)

    extra = rank - 12
    spot = jnp.where(rank >= 12, ((own >> 4) & 1) * 64 + (own & 15) * 4 + (extra & 3), -1)
    place = hit(iota((128, 1024), 0) == spot)
    group = (own >> 5) * 8 + (extra >> 2)
    half = iota((16, 128), 1) < 64
    for g in range(2):
        left = jnp.concatenate(
            [jnp.where(group == g * 8 + h, sources, 0.0).astype(BF16) for h in range(8)], axis=0)
        more = dot(left, place, NT)
        for h in range(8):
            r0, r1 = more[h * 32:h * 32 + 16], more[h * 32 + 16:h * 32 + 32]
            even = jnp.where(half, r0, pltpu.roll(r1, 64, 1))
            odd = jnp.where(half, pltpu.roll(r0, 64, 1), r1)
            at = ((2 * g) * 8 + h) * 16
            ex_ref[at:at + 16, :] = even.astype(BF16)
            at = ((2 * g + 1) * 8 + h) * 16
            ex_ref[at:at + 16, :] = odd.astype(BF16)

    wf[...] = w_ref[...].astype(F32)
    counts = jnp.sum(jnp.where(owner_ref[...] == panel, 1.0, 0.0), axis=1, keepdims=True)
    heavy = jnp.sum(jnp.where(counts > 28.0, iota((8, 1), 0).astype(F32), 0.0), axis=0, keepdims=True).astype(I32)
    slot_lane = iota((1, 512), 1)
    relay, quant, slot = slot_lane >> 6, (slot_lane >> 4) & 3, slot_lane & 15
    panel_at = jnp.where(slot < 12, 12 * relay + jnp.where(relay > heavy, 32, 0) + slot,
                         12 * heavy + 4 * relay + slot)
    target = quant * 128 + panel_at
    mover = hit(iota((512, 512), 0) == target)
    for k in range(4):
        rows = jnp.concatenate([wf[pl.ds(k * 4 + q, 128, stride=16), :].astype(BF16) for q in range(4)], axis=1)
        w2_ref[k * 128:k * 128 + 128, :] = dot(rows, mover, NN).astype(BF16)


def pick(donor, elem, coords, owner, weights):
    vmem = pl.BlockSpec(memory_space=pltpu.VMEM)
    return pl.pallas_call(
        pick_kernel,
        out_shape=(
            jax.ShapeDtypeStruct((256, 128), BF16),
            jax.ShapeDtypeStruct((512, 128), BF16),
            jax.ShapeDtypeStruct((512, 512), BF16),
        ),
        in_specs=[vmem] * 5,
        out_specs=(vmem, vmem, vmem),
        scratch_shapes=[
            pltpu.VMEM((1000, 1024), F32),
            pltpu.VMEM((128, 1024), BF16),
            pltpu.VMEM((8, 32, 128), F32),
            pltpu.VMEM((2048, 128), F32),
        ],
        compiler_params=pltpu.CompilerParams(vmem_limit_bytes=48 * 2**20),
    )(donor, elem, coords, owner, weights)


def mix_pair(a, b, low):
    return jnp.where(low, a, pltpu.roll(b, 4, 0)), jnp.where(low, pltpu.roll(a, 4, 0), b)


def move_kernel(base_ref, ex_ref, w2_ref, off_ref, out_ref,
                base_in, ex_in, msg, held, wide, part, part_b, part_in, line, line_in,
                base_s, base_r, ex_s, ex_r, z_s, z_r, o_s, o_r, px_s, px_r, pz_s, pz_r, own_sem):
    panel = lax.axis_index("panel")
    b = lax.axis_index("obs")
    x = panel // NZ
    z = panel % NZ
    me = x * NB + b

    def at(px, pz, pb):
        return {"panel": px * NZ + pz, "obs": pb}

    def remote(src, dst, send, recv, device):
        return pltpu.make_async_remote_copy(
            src_ref=src, dst_ref=dst, send_sem=send, recv_sem=recv,
            device_id=device, device_id_type=pl.DeviceIdType.MESH)

    barrier = pltpu.get_barrier_semaphore()

    def greet(i, c):
        slot = (me + i) % 32
        pl.semaphore_signal(barrier, inc=1, device_id=at(slot // NB, z, slot % NB),
                            device_id_type=pl.DeviceIdType.MESH)
        return c

    def greet_z(i, c):
        pl.semaphore_signal(barrier, inc=1, device_id=at(x, (z + i) % NZ, b),
                            device_id_type=pl.DeviceIdType.MESH)
        return c

    lax.fori_loop(1, 32, greet, 0)
    lax.fori_loop(1, NZ, greet_z, 0)
    pl.semaphore_wait(barrier, 46)

    def base_copy(px, source):
        return remote(base_ref.at[pl.ds(px * 64, 64)], base_in.at[source], base_s.at[px], base_r.at[source],
                      at(px, z, b))

    def ex_copy(slot, source):
        return remote(ex_ref.at[pl.ds(slot * 16, 16)], ex_in.at[source], ex_s.at[slot], ex_r.at[source],
                      at(slot // NB, z, slot % NB))

    def base_start(i, c):
        base_copy((x + i) % NX, x).start()
        return c

    def ex_start(i, c):
        ex_copy((me + i) % 32, me).start()
        return c

    lax.fori_loop(1, NX, base_start, 0)
    lax.fori_loop(1, 32, ex_start, 0)
    own_base = pltpu.make_async_copy(base_ref.at[pl.ds(x * 64, 64)], base_in.at[x], own_sem.at[0])
    own_ex = pltpu.make_async_copy(ex_ref.at[pl.ds(me * 16, 16)], ex_in.at[me], own_sem.at[1])
    own_base.start()
    own_ex.start()
    wide[:, 0:FRONT, :] = jnp.zeros((4, FRONT, 128), F32)
    own_base.wait()
    own_ex.wait()

    def base_wait(i, c):
        base_copy((x + i) % NX, (x + i) % NX).wait_recv()
        return c

    def ex_wait(i, c):
        ex_copy((me + i) % 32, (me + i) % 32).wait_recv()
        return c

    lax.fori_loop(1, NX, base_wait, 0)
    lax.fori_loop(1, 32, ex_wait, 0)

    low = iota((8, 128), 0) < 4
    lane = iota((8, 128), 1)
    sums = []
    for px in range(NX):
        total = ex_in[px * NB].astype(F32)
        for pb in range(1, NB):
            total = total + ex_in[px * NB + pb].astype(F32)
        sums.append(total)
    quants = []
    for v in range(2):
        rows = slice(v * 8, v * 8 + 8)
        e01, o01 = mix_pair(sums[0][rows], sums[1][rows], low)
        e23, o23 = mix_pair(sums[2][rows], sums[3][rows], low)
        quants += [(e01, e23), (o01, o23)]
    bases = [base_in[px].astype(F32) for px in range(NX)]
    masks = [((lane & 63) >= 16 * q + 12) & ((lane & 63) < 16 * q + 16) for q in range(4)]
    for v in range(8):
        rows = slice(v * 8, v * 8 + 8)
        e01, o01 = mix_pair(bases[0][rows], bases[1][rows], low)
        e23, o23 = mix_pair(bases[2][rows], bases[3][rows], low)
        for pz, halves in ((2 * v, (e01, e23)), (2 * v + 1, (o01, o23))):
            done = []
            for h in range(2):
                value = halves[h]
                for q in range(4):
                    shift = (16 * q + 12 - 4 * pz) % 128
                    value = jnp.where(masks[q], pltpu.roll(quants[q][h], shift, 1), value)
                done.append(value)
            msg[pz] = jnp.concatenate(done, axis=0).astype(BF16)

    def z_copy(pz, source):
        return remote(msg.at[pz], held.at[b, pl.ds(source * 16, 16)], z_s.at[pz], z_r.at[source], at(x, pz, b))

    def z_start(i, c):
        z_copy((z + i) % NZ, z).start()
        return c

    def z_wait(i, c):
        z_copy((z + i) % NZ, (z + i) % NZ).wait_recv()
        return c

    lax.fori_loop(1, NZ, z_start, 0)
    own_z = pltpu.make_async_copy(msg.at[z], held.at[b, pl.ds(z * 16, 16)], own_sem.at[0])
    own_z.start()
    own_z.wait()
    lax.fori_loop(1, NZ, z_wait, 0)

    def o_copy(pb, source):
        return remote(held.at[source], held.at[source], o_s.at[pb], o_r.at[source], at(x, z, pb))

    def o_start(i, c):
        o_copy((b + i) % NB, b).start()
        return c

    def o_wait(i, c):
        o_copy((b + i) % NB, (b + i) % NB).wait_recv()
        return c

    lax.fori_loop(1, NB, o_start, 0)
    lax.fori_loop(1, NB, o_wait, 0)

    low_wide = iota((8, 512), 0) < 4
    for parity in range(2):
        cols = slice(parity * 64, parity * 64 + 64)
        left = jnp.concatenate([held[pb][:, cols] for pb in range(NB)], axis=1)
        y = dot(left, w2_ref[...], NT)
        for xp in range(2):
            evens, odds = [], []
            for v in range(8):
                first = y[v * 32 + xp * 8:v * 32 + xp * 8 + 8]
                second = y[v * 32 + 16 + xp * 8:v * 32 + 16 + xp * 8 + 8]
                even, odd = mix_pair(first, second, low_wide)
                evens.append(even)
                odds.append(odd)
            even, odd = jnp.concatenate(evens, axis=0), jnp.concatenate(odds, axis=0)
            for k in range(4):
                cols = slice(k * 128, k * 128 + 128)
                wide[k, pl.ds(FRONT + 256 * xp + parity, 64, stride=2), :] = even[:, cols]
                wide[k, pl.ds(FRONT + 256 * xp + 128 + parity, 64, stride=2), :] = odd[:, cols]
    delay = off_ref[0, 0]
    total = wide[0, pl.ds(FRONT - delay, TW), :]
    for k in range(1, 4):
        total = total + wide[k, pl.ds(FRONT - delay - k, TW), :]
    part[...] = total
    part_b[...] = total.astype(BF16).reshape(NX, 128, 128)

    def px_copy(px, source):
        return remote(part_b.at[px], part_in.at[source], px_s.at[px], px_r.at[source], at(px, z, b))

    def px_start(i, c):
        px_copy((x + i) % NX, x).start()
        return c

    lax.fori_loop(1, NX, px_start, 0)
    acc = part[pl.ds(x * 128, 128), :]
    for i in range(1, NX):
        source = (x + i) % NX
        px_copy(source, source).wait_recv()
        acc = acc + part_in[source].astype(F32)
    line[...] = acc

    def pz_copy(pz, source):
        return remote(line.at[pl.ds(pz * 8, 8)], line_in.at[source], pz_s.at[pz], pz_r.at[source], at(x, pz, b))

    def pz_start(i, c):
        pz_copy((z + i) % NZ, z).start()
        return c

    lax.fori_loop(1, NZ, pz_start, 0)
    acc = line[pl.ds(z * 8, 8), :]
    for i in range(1, NZ):
        source = (z + i) % NZ
        pz_copy(source, source).wait_recv()
        acc = acc + line_in[source]
    out_ref[...] = acc

    def base_end(i, c):
        base_copy((x + i) % NX, x).wait_send()
        px_copy((x + i) % NX, x).wait_send()
        return c

    def ex_end(i, c):
        ex_copy((me + i) % 32, me).wait_send()
        return c

    def z_end(i, c):
        z_copy((z + i) % NZ, z).wait_send()
        pz_copy((z + i) % NZ, z).wait_send()
        return c

    def o_end(i, c):
        o_copy((b + i) % NB, b).wait_send()
        return c

    lax.fori_loop(1, NX, base_end, 0)
    lax.fori_loop(1, 32, ex_end, 0)
    lax.fori_loop(1, NZ, z_end, 0)
    lax.fori_loop(1, NB, o_end, 0)


def move(base, ex, w2, offsets):
    vmem = pl.BlockSpec(memory_space=pltpu.VMEM)
    dma = pltpu.SemaphoreType.DMA
    return pl.pallas_call(
        move_kernel,
        out_shape=jax.ShapeDtypeStruct((8, 128), F32),
        in_specs=[vmem, vmem, vmem, pl.BlockSpec(memory_space=pltpu.SMEM)],
        out_specs=vmem,
        scratch_shapes=[
            pltpu.VMEM((NX, 64, 128), BF16),
            pltpu.VMEM((NX * NB, 16, 128), BF16),
            pltpu.VMEM((NZ, 16, 128), BF16),
            pltpu.VMEM((NB, 256, 128), BF16),
            pltpu.VMEM((4, FRONT + TW, 128), F32),
            pltpu.VMEM((TW, 128), F32),
            pltpu.VMEM((NX, 128, 128), BF16),
            pltpu.VMEM((NX, 128, 128), BF16),
            pltpu.VMEM((128, 128), F32),
            pltpu.VMEM((NZ, 8, 128), F32),
            dma((NX,)), dma((NX,)), dma((32,)), dma((32,)), dma((NZ,)), dma((NZ,)),
            dma((NB,)), dma((NB,)), dma((NX,)), dma((NX,)), dma((NZ,)), dma((NZ,)), dma((2,)),
        ],
        compiler_params=pltpu.CompilerParams(
            collective_id=0, has_side_effects=True, vmem_limit_bytes=48 * 2**20),
    )(base, ex, w2, offsets)


def body(donor, donor_elem, local_coords, owner, weights, offsets):
    base, ex, w2 = pick(
        donor.reshape(4000, 128),
        donor_elem.reshape(1, 1024),
        local_coords,
        owner.reshape(8, 1024),
        weights.reshape(2048, 128),
    )
    return move(base, ex, w2, offsets)


def solution(mesh):
    return jax.shard_map(
        body,
        mesh=mesh,
        in_specs=(
            P("panel", None, None, "obs"),
            P("obs"),
            P(None, "obs"),
            P(),
            P("obs", None, None, "panel"),
            P("obs", "panel"),
        ),
        out_specs=P("panel", "obs"),
        check_vma=False,
    )
```

```python
import jax
import jax.numpy as jnp
from jax import lax
from jax.experimental import pallas as pl
from jax.experimental.pallas import tpu as pltpu
from jax.sharding import PartitionSpec as P

F32 = jnp.float32
BF16 = jnp.bfloat16
I32 = jnp.int32
SPOTS = (-1.0, -0.5, 0.0, 0.5, 1.0)
NX = 4
NZ = 16
NB = 8
FRONT = 264
TW = 512
NT = (((1,), (1,)), ((), ()))
NN = (((1,), (0,)), ((), ()))
MESH = pl.DeviceIdType.MESH
GROUPS = ((0, 112), (112, 96), (208, 48))
GROUP_ENDS = (7, 13, 16)
OBS_ORDER = (4, 3, 5, 2, 6, 7, 1)


def iota(shape, axis):
    return lax.broadcasted_iota(I32, shape, axis)


def dot(a, b, dims):
    return lax.dot_general(a, b, dims, preferred_element_type=F32)


def hit(cond):
    return jnp.where(cond, 1.0, 0.0).astype(BF16)


def flat_row(tiles):
    return jnp.concatenate([tiles[t:t + 1] for t in range(8)], axis=1)


def mix_pair(a, b, low):
    return jnp.where(low, a, pltpu.roll(b, 4, 0)), jnp.where(low, pltpu.roll(a, 4, 0), b)


def fill_table(coord_ref, table):
    def table_step(tile, carry):
        lanes = pl.ds(pl.multiple_of(tile * 128, 128), 128)
        factors = []
        for direction in range(3):
            x = jnp.broadcast_to(coord_ref[direction:direction + 1, lanes], (8, 128))
            column = []
            for one in range(5):
                value = None
                for two in range(5):
                    if two != one:
                        term = (x - SPOTS[two]) * (1.0 / (SPOTS[one] - SPOTS[two]))
                        value = term if value is None else value * term
                column.append(value)
            factors.append(column)
        low = iota((8, 128), 0) < 4
        pairs = [[fa * fb for fb in factors[1]] for fa in factors[0]]
        nodes = [pairs[n // 25][(n // 5) % 5] * factors[2][n % 5] for n in range(125)]
        for j in range(125):
            table[8 * j:8 * j + 8, lanes] = jnp.where(low, nodes[(2 * j) % 125], nodes[(2 * j + 1) % 125])
        return carry

    lax.fori_loop(0, 8, table_step, 0)


def fill_sources(donor, hot, table, src):
    def point_step(tile, carry):
        lanes = pl.ds(pl.multiple_of(tile * 256, 256), 256)
        for part in range(2):
            picked = dot(donor[part * 2000:part * 2000 + 2000, :], hot[:, lanes], NN)
            for half in range(2):
                prod = picked[half * 1000:half * 1000 + 1000] * table[:, lanes]
                prod = prod.reshape(125, 8, 256)
                first = jnp.sum(prod[:62], axis=0)
                last = jnp.sum(prod[63:], axis=0)
                mid = prod[62]
                step = 16 * part + 2 * half
                even = first[:4] + first[4:] + mid[:4]
                odd = last[:4] + last[4:] + mid[4:]
                for side in range(2):
                    cols = slice(side * 128, side * 128 + 128)
                    src[2 * tile + side, pl.ds(step, 4, stride=4), :] = even[:, cols]
                    src[2 * tile + side, pl.ds(step + 1, 4, stride=4), :] = odd[:, cols]
        return carry

    lax.fori_loop(0, 4, point_step, 0)


def rank_points(own):
    member = iota((64, 1024), 0) == own
    member_f = jnp.where(member, 1.0, 0.0)
    member_b = member_f.astype(BF16)
    upper = hit(iota((128, 128), 0) < iota((128, 128), 1))
    ones = jnp.ones((128, 128), BF16)
    carry = jnp.zeros((64, 128), F32)
    ranks = []
    for tile in range(8):
        cols = slice(tile * 128, tile * 128 + 128)
        below = dot(member_b[:, cols], upper, NN) + carry
        ranks.append(jnp.sum(member_f[:, cols] * below, axis=0, keepdims=True))
        carry = carry + dot(member_b[:, cols], ones, NN)
    return jnp.concatenate(ranks, axis=1).astype(I32)


def group_base(sources, own, rank, base_ref):
    spot = jnp.where(rank < 12, (own & 7) * 16 + rank, -1)
    place = hit(iota((128, 1024), 0) == spot)
    group = own >> 3
    left = jnp.concatenate([jnp.where(group == g, sources, 0.0).astype(BF16) for g in range(8)], axis=0)
    grouped = dot(left, place, NT)
    row = iota((32, 128), 0)
    lane = iota((32, 128), 1)
    for g in range(8):
        x = grouped[g * 32:g * 32 + 32]
        for k in range(3):
            r, l = 4 << k, 16 << k
            rbit, lbit = (row >> (2 + k)) & 1, (lane >> (4 + k)) & 1
            up = pltpu.roll(pltpu.roll(x, 32 - r, 0), l, 1)
            down = pltpu.roll(pltpu.roll(x, r, 0), 128 - l, 1)
            x = jnp.where(rbit == lbit, x, jnp.where(rbit == 0, up, down))
        base_ref[g * 32:g * 32 + 32, :] = x.astype(BF16)


def group_extra(sources, own, rank, ex_ref):
    extra = rank - 12
    spot = jnp.where(rank >= 12, ((own >> 4) & 1) * 64 + (own & 15) * 4 + (extra & 3), -1)
    place = hit(iota((128, 1024), 0) == spot)
    group = (own >> 5) * 8 + (extra >> 2)
    half = iota((16, 128), 1) < 64
    for g in range(2):
        left = jnp.concatenate(
            [jnp.where(group == g * 8 + h, sources, 0.0).astype(BF16) for h in range(8)], axis=0)
        more = dot(left, place, NT)
        for h in range(8):
            r0, r1 = more[h * 32:h * 32 + 16], more[h * 32 + 16:h * 32 + 32]
            even = jnp.where(half, r0, pltpu.roll(r1, 64, 1))
            odd = jnp.where(half, pltpu.roll(r0, 64, 1), r1)
            at = ((2 * g) * 8 + h) * 16
            ex_ref[at:at + 16, :] = even.astype(BF16)
            at = ((2 * g + 1) * 8 + h) * 16
            ex_ref[at:at + 16, :] = odd.astype(BF16)


def order_weights(w_ref, owner_ref, panel, wf, w2_ref):
    wf[...] = w_ref[...].astype(F32)
    same = jnp.where(owner_ref[...] == panel, 1.0, 0.0)
    heavy = jnp.zeros((1, 1), F32)
    for block in range(1, 8):
        count = jnp.sum(jnp.sum(same[block * 8:block * 8 + 8], axis=0, keepdims=True), axis=1, keepdims=True)
        heavy = heavy + jnp.where(count > 28.0, float(block), 0.0)
    heavy = heavy.astype(I32)
    slot_lane = iota((1, 512), 1)
    relay, quant, slot = slot_lane >> 6, (slot_lane >> 4) & 3, slot_lane & 15
    panel_at = jnp.where(slot < 12, 12 * relay + jnp.where(relay > heavy, 32, 0) + slot,
                         12 * heavy + 4 * relay + slot)
    mover = hit(iota((512, 512), 0) == quant * 128 + panel_at)
    for k in range(4):
        rows = jnp.concatenate([wf[pl.ds(k * 4 + q, 128, stride=16), :].astype(BF16) for q in range(4)], axis=1)
        w2_ref[k * 128:k * 128 + 128, :] = dot(rows, mover, NN).astype(BF16)


def fill_messages(base_in, ex_in, msg):
    low = iota((8, 128), 0) < 4
    lane = iota((8, 128), 1)
    sums = []
    for px in range(NX):
        total = ex_in[px * NB].astype(F32)
        for pb in range(1, NB):
            total = total + ex_in[px * NB + pb].astype(F32)
        sums.append(total)
    quants = []
    for v in range(2):
        rows = slice(v * 8, v * 8 + 8)
        e01, o01 = mix_pair(sums[0][rows], sums[1][rows], low)
        e23, o23 = mix_pair(sums[2][rows], sums[3][rows], low)
        quants += [(e01, e23), (o01, o23)]
    bases = [base_in[px].astype(F32) for px in range(NX)]
    masks = [((lane & 63) >= 16 * q + 12) & ((lane & 63) < 16 * q + 16) for q in range(4)]
    for v in range(8):
        rows = slice(v * 8, v * 8 + 8)
        e01, o01 = mix_pair(bases[0][rows], bases[1][rows], low)
        e23, o23 = mix_pair(bases[2][rows], bases[3][rows], low)
        for pz, halves in ((2 * v, (e01, e23)), (2 * v + 1, (o01, o23))):
            done = []
            for h in range(2):
                value = halves[h]
                for q in range(4):
                    shift = (16 * q + 12 - 4 * pz) % 128
                    value = jnp.where(masks[q], pltpu.roll(quants[q][h], shift, 1), value)
                done.append(value)
            msg[pz] = jnp.concatenate(done, axis=0).astype(BF16)


def kernel(donor_hbm, elem_ref, coord_ref, owner_ref, w_hbm, off_ref, out_ref,
           donor, weights, table, hot, src, wf, w2, base_out, ex_out,
           base_in, ex_in, msg, held, wide, part, part_b, part_in, line, line_in,
           base_s, base_r, ex_s, ex_r, z_s, z_r, o_s, o_r, px_s, px_r, pz_s, pz_r, own_sem):
    panel = lax.axis_index("panel")
    b = lax.axis_index("obs")
    x = panel // NZ
    z = panel % NZ
    me = x * NB + b

    def at(px, pz, pb):
        return {"panel": px * NZ + pz, "obs": pb}

    def remote(src_ref, dst_ref, send, recv, device):
        return pltpu.make_async_remote_copy(
            src_ref=src_ref, dst_ref=dst_ref, send_sem=send, recv_sem=recv,
            device_id=device, device_id_type=MESH)

    donor_copy = pltpu.make_async_copy(donor_hbm, donor, own_sem.at[0])
    weight_copy = pltpu.make_async_copy(w_hbm, weights, own_sem.at[1])
    donor_copy.start()
    weight_copy.start()
    barrier = pltpu.get_barrier_semaphore()

    def greet(i, c):
        slot = (me + i) % 32
        pl.semaphore_signal(barrier, inc=1, device_id=at(slot // NB, z, slot % NB), device_id_type=MESH)
        return c

    def greet_z(i, c):
        pl.semaphore_signal(barrier, inc=1, device_id=at(x, (z + i) % NZ, b), device_id_type=MESH)
        return c

    lax.fori_loop(1, NZ, greet_z, 0)
    lax.fori_loop(1, 32, greet, 0)

    fill_table(coord_ref, table)
    hot[...] = hit(iota((128, 1024), 0) == elem_ref[...] - b * 128)
    own = flat_row(owner_ref[pl.ds(b * 8, 8), :])
    rank = rank_points(own)
    donor_copy.wait()
    fill_sources(donor, hot, table, src)
    sources = jnp.concatenate([src[tile] for tile in range(8)], axis=1).astype(BF16).astype(F32)
    group_extra(sources, own, rank, ex_out)
    group_base(sources, own, rank, base_out)
    pl.semaphore_wait(barrier, 46)

    def base_copy(px, source):
        return remote(base_out.at[pl.ds(px * 64, 64)], base_in.at[source], base_s.at[px], base_r.at[source],
                      at(px, z, b))

    def ex_copy(slot, source):
        return remote(ex_out.at[pl.ds(slot * 16, 16)], ex_in.at[source], ex_s.at[slot], ex_r.at[source],
                      at(slot // NB, z, slot % NB))

    def ex_start(j, c):
        ex_copy((me + 12 + j + j // 20) % 32, me).start()
        return c

    for i in (2, 1, 3):
        base_copy((x + i) % NX, x).start()
    lax.fori_loop(0, 31, ex_start, 0)
    weight_copy.wait()
    own_base = pltpu.make_async_copy(base_out.at[pl.ds(x * 64, 64)], base_in.at[x], own_sem.at[0])
    own_ex = pltpu.make_async_copy(ex_out.at[pl.ds(me * 16, 16)], ex_in.at[me], own_sem.at[1])
    own_base.start()
    own_ex.start()
    wide[:, 0:FRONT, :] = jnp.zeros((4, FRONT, 128), F32)
    order_weights(weights, owner_ref, panel, wf, w2)
    own_base.wait()
    own_ex.wait()

    def ex_wait(i, c):
        ex_copy((me + i) % 32, (me + i) % 32).wait_recv()
        return c

    for i in (1, 3, 2):
        base_copy((x + i) % NX, (x + i) % NX).wait_recv()
    lax.fori_loop(1, 32, ex_wait, 0)
    fill_messages(base_in, ex_in, msg)

    def away(i):
        h = (i + 1) // 2
        return h + (1 - i % 2) * (NZ - 2 * h)

    def z_copy(i):
        pz = (z + NZ - away(i)) % NZ
        return remote(msg.at[pz], held.at[b, pl.ds(i * 16, 16)], z_s.at[i], z_r.at[i], at(x, pz, b))

    def z_start(i, c):
        z_copy(NZ - i).start()
        return c

    def z_wait(i, c):
        z_copy(i).wait_recv()
        return c

    lax.fori_loop(1, NZ, z_start, 0)
    own_z = pltpu.make_async_copy(msg.at[z], held.at[b, pl.ds(0, 16)], own_sem.at[0])
    own_z.start()
    own_z.wait()

    def o_copy(g, pb, source):
        rows = pl.ds(*GROUPS[g])
        return remote(held.at[source, rows], held.at[source, rows], o_s.at[g * NB + pb], o_r.at[g * NB + source],
                      at(x, z, pb))

    begin = 1
    for g in range(3):
        lax.fori_loop(begin, GROUP_ENDS[g], z_wait, 0)
        begin = GROUP_ENDS[g]
        for i in OBS_ORDER:
            o_copy(g, (b + i) % NB, b).start()
    for g in range(3):
        for i in range(1, NB):
            o_copy(g, (b + i) % NB, (b + i) % NB).wait_recv()

    low_wide = iota((8, 512), 0) < 4
    halves = []
    for side in range(2):
        cols = slice(side * 64, side * 64 + 64)
        left = jnp.concatenate([held[pb][:, cols] for pb in range(NB)], axis=1)
        halves.append(dot(left, w2[...], NT))
    for i in range(NZ):
        time = FRONT + 8 * ((z + away(i)) % NZ)
        for xp in range(2):
            rows = slice(i * 16 + xp * 8, i * 16 + xp * 8 + 8)
            pair = mix_pair(halves[0][rows], halves[1][rows], low_wide)
            for side in range(2):
                start = pl.multiple_of(time + 128 * (2 * xp + side), 8)
                for k in range(4):
                    wide[k, pl.ds(start, 8), :] = pair[side][:, k * 128:k * 128 + 128]
    delay = off_ref[0, 0]
    total = wide[0, pl.ds(FRONT - delay, TW), :]
    for k in range(1, 4):
        total = total + wide[k, pl.ds(FRONT - delay - k, TW), :]
    part[...] = total
    part_b[...] = total.astype(BF16).reshape(NX, 128, 128)

    def px_copy(i):
        px = (x + NX - i) % NX
        return remote(part_b.at[px], part_in.at[i], px_s.at[i], px_r.at[i], at(px, z, b))

    for i in (2, 1, 3):
        px_copy(i).start()
    acc = part[pl.ds(pl.multiple_of(x * 128, 128), 128), :]
    for i in (1, 3, 2):
        px_copy(i).wait_recv()
        acc = acc + part_in[i].astype(F32)
    line[...] = acc

    def pz_copy(i):
        pz = (z + NZ - away(i)) % NZ
        return remote(line.at[pl.ds(pz * 8, 8)], line_in.at[i], pz_s.at[i], pz_r.at[i], at(x, pz, b))

    def pz_start(i, c):
        pz_copy(NZ - i).start()
        return c

    def pz_wait(i, c):
        pz_copy(i).wait_recv()
        return c

    lax.fori_loop(1, NZ, pz_start, 0)

    def ex_end(i, c):
        ex_copy((me + i) % 32, me).wait_send()
        return c

    def z_end(i, c):
        z_copy(i).wait_send()
        return c

    def pz_end(i, c):
        pz_copy(i).wait_send()
        return c

    for i in range(1, NX):
        base_copy((x + i) % NX, x).wait_send()
        px_copy(i).wait_send()
    lax.fori_loop(1, 32, ex_end, 0)
    lax.fori_loop(1, NZ, z_end, 0)
    for g in range(3):
        for i in range(1, NB):
            o_copy(g, (b + i) % NB, b).wait_send()
    lax.fori_loop(1, NZ, pz_end, 0)

    acc = line[pl.ds(pl.multiple_of(z * 8, 8), 8), :]
    lax.fori_loop(1, NZ, pz_wait, 0)
    for i in range(1, NZ):
        acc = acc + line_in[i]
    out_ref[...] = acc


def body(donor, donor_elem, local_coords, owner, weights, offsets):
    vmem = pl.BlockSpec(memory_space=pltpu.VMEM)
    anywhere = pl.BlockSpec(memory_space=pl.ANY)
    dma = pltpu.SemaphoreType.DMA
    return pl.pallas_call(
        kernel,
        out_shape=jax.ShapeDtypeStruct((8, 128), F32),
        in_specs=[anywhere, vmem, vmem, vmem, anywhere, pl.BlockSpec(memory_space=pltpu.SMEM)],
        out_specs=vmem,
        scratch_shapes=[
            pltpu.VMEM((4000, 128), BF16),
            pltpu.VMEM((2048, 128), BF16),
            pltpu.VMEM((1000, 1024), F32),
            pltpu.VMEM((128, 1024), BF16),
            pltpu.VMEM((8, 32, 128), F32),
            pltpu.VMEM((2048, 128), F32),
            pltpu.VMEM((512, 512), BF16),
            pltpu.VMEM((256, 128), BF16),
            pltpu.VMEM((512, 128), BF16),
            pltpu.VMEM((NX, 64, 128), BF16),
            pltpu.VMEM((NX * NB, 16, 128), BF16),
            pltpu.VMEM((NZ, 16, 128), BF16),
            pltpu.VMEM((NB, 256, 128), BF16),
            pltpu.VMEM((4, FRONT + TW, 128), F32),
            pltpu.VMEM((TW, 128), F32),
            pltpu.VMEM((NX, 128, 128), BF16),
            pltpu.VMEM((NX, 128, 128), BF16),
            pltpu.VMEM((128, 128), F32),
            pltpu.VMEM((NZ, 8, 128), F32),
            dma((NX,)), dma((NX,)), dma((32,)), dma((32,)), dma((NZ,)), dma((NZ,)),
            dma((3 * NB,)), dma((3 * NB,)), dma((NX,)), dma((NX,)), dma((NZ,)), dma((NZ,)), dma((2,)),
        ],
        compiler_params=pltpu.CompilerParams(
            collective_id=0, has_side_effects=True, vmem_limit_bytes=60 * 2**20),
    )(
        donor.reshape(4000, 128),
        donor_elem.reshape(1, 1024),
        local_coords,
        owner.reshape(64, 128),
        weights.reshape(2048, 128),
        offsets,
    )


def solution(mesh):
    return jax.shard_map(
        body,
        mesh=mesh,
        in_specs=(
            P("panel", None, None, "obs"),
            P("obs"),
            P(None, "obs"),
            P(),
            P("obs", None, None, "panel"),
            P("obs", "panel"),
        ),
        out_specs=P("panel", "obs"),
        check_vma=False,
    )
```

```python
import jax
import jax.numpy as jnp
from jax import lax
from jax.experimental import pallas as pl
from jax.experimental.pallas import tpu as pltpu
from jax.sharding import PartitionSpec as P

F32 = jnp.float32
BF16 = jnp.bfloat16
I32 = jnp.int32
SPOTS = (-1.0, -0.5, 0.0, 0.5, 1.0)
NX = 4
NZ = 16
NB = 8
FRONT = 264
TW = 512
NT = (((1,), (1,)), ((), ()))
NN = (((1,), (0,)), ((), ()))
MESH = pl.DeviceIdType.MESH
GROUPS = ((0, 112), (112, 96), (208, 48))
GROUP_ENDS = (7, 13, 16)
AWAY = (0, 1, 15, 2, 14, 3, 13, 4, 12, 5, 11, 6, 10, 7, 9, 8)
Z_FAR = AWAY[:0:-1]
OBS_FAR = (5, 4, 3, 7, 2, 6, 1, 0)
BACK = (0, 1, 6, 7, 4, 5, 2, 3)


def iota(shape, axis):
    return lax.broadcasted_iota(I32, shape, axis)


def dot(a, b, dims):
    return lax.dot_general(a, b, dims, preferred_element_type=F32)


def hit(cond):
    return jnp.where(cond, 1.0, 0.0).astype(BF16)


def flat_row(tiles):
    return jnp.concatenate([tiles[t:t + 1] for t in range(8)], axis=1)


def mix_pair(a, b, low):
    return jnp.where(low, a, pltpu.roll(b, 4, 0)), jnp.where(low, pltpu.roll(a, 4, 0), b)


def fill_table(coord_ref, table, greet):
    def table_step(tile):
        lanes = pl.ds(pl.multiple_of(tile * 128, 128), 128)
        factors = []
        for direction in range(3):
            x = jnp.broadcast_to(coord_ref[direction:direction + 1, lanes], (8, 128))
            column = []
            for one in range(5):
                value = None
                for two in range(5):
                    if two != one:
                        term = (x - SPOTS[two]) * (1.0 / (SPOTS[one] - SPOTS[two]))
                        value = term if value is None else value * term
                column.append(value)
            factors.append(column)
        low = iota((8, 128), 0) < 4
        pairs = [[fa * fb for fb in factors[1]] for fa in factors[0]]
        nodes = [pairs[n // 25][(n // 5) % 5] * factors[2][n % 5] for n in range(125)]
        for j in range(125):
            table[8 * j:8 * j + 8, lanes] = jnp.where(low, nodes[(2 * j) % 125], nodes[(2 * j + 1) % 125])

    def table_loop(tile, carry):
        for k in range(4):
            greet(4 * tile + k)
        table_step(tile)
        return carry

    lax.fori_loop(1, 8, table_loop, 0)
    for k in range(1, 4):
        greet(k)
    table_step(0)


def fill_sources(donor, hot, table, src):
    def point_step(tile, carry):
        lanes = pl.ds(pl.multiple_of(tile * 256, 256), 256)
        for part in range(2):
            picked = dot(donor[part * 2000:part * 2000 + 2000, :], hot[:, lanes], NN)
            for half in range(2):
                prod = picked[half * 1000:half * 1000 + 1000] * table[:, lanes]
                prod = prod.reshape(125, 8, 256)
                first = jnp.sum(prod[:62], axis=0)
                last = jnp.sum(prod[63:], axis=0)
                mid = prod[62]
                step = 16 * part + 2 * half
                even = first[:4] + first[4:] + mid[:4]
                odd = last[:4] + last[4:] + mid[4:]
                for side in range(2):
                    cols = slice(side * 128, side * 128 + 128)
                    src[2 * tile + side, pl.ds(step, 4, stride=4), :] = even[:, cols]
                    src[2 * tile + side, pl.ds(step + 1, 4, stride=4), :] = odd[:, cols]
        return carry

    lax.fori_loop(0, 4, point_step, 0)


def rank_points(own):
    member = iota((64, 1024), 0) == own
    member_f = jnp.where(member, 1.0, 0.0)
    member_b = member_f.astype(BF16)
    upper = hit(iota((128, 128), 0) < iota((128, 128), 1))
    ones = jnp.ones((128, 128), BF16)
    carry = jnp.zeros((64, 128), F32)
    ranks = []
    for tile in range(8):
        cols = slice(tile * 128, tile * 128 + 128)
        below = dot(member_b[:, cols], upper, NN) + carry
        ranks.append(jnp.sum(member_f[:, cols] * below, axis=0, keepdims=True))
        carry = carry + dot(member_b[:, cols], ones, NN)
    return jnp.concatenate(ranks, axis=1).astype(I32)


def group_base(sources, own, rank, base_ref):
    spot = jnp.where(rank < 12, (own & 7) * 16 + rank, -1)
    place = hit(iota((128, 1024), 0) == spot)
    group = own >> 3
    left = jnp.concatenate([jnp.where(group == g, sources, 0.0).astype(BF16) for g in range(8)], axis=0)
    grouped = dot(left, place, NT)
    row = iota((32, 128), 0)
    lane = iota((32, 128), 1)
    for g in range(8):
        x = grouped[g * 32:g * 32 + 32]
        for k in range(3):
            r, l = 4 << k, 16 << k
            rbit, lbit = (row >> (2 + k)) & 1, (lane >> (4 + k)) & 1
            up = pltpu.roll(pltpu.roll(x, 32 - r, 0), l, 1)
            down = pltpu.roll(pltpu.roll(x, r, 0), 128 - l, 1)
            x = jnp.where(rbit == lbit, x, jnp.where(rbit == 0, up, down))
        base_ref[g * 32:g * 32 + 32, :] = x.astype(BF16)


def group_extra(sources, own, rank, ex_ref):
    extra = rank - 12
    spot = jnp.where(rank >= 12, ((own >> 4) & 1) * 64 + (own & 15) * 4 + (extra & 3), -1)
    place = hit(iota((128, 1024), 0) == spot)
    group = (own >> 5) * 8 + (extra >> 2)
    half = iota((16, 128), 1) < 64
    for g in range(2):
        left = jnp.concatenate(
            [jnp.where(group == g * 8 + h, sources, 0.0).astype(BF16) for h in range(8)], axis=0)
        more = dot(left, place, NT)
        for h in range(8):
            r0, r1 = more[h * 32:h * 32 + 16], more[h * 32 + 16:h * 32 + 32]
            even = jnp.where(half, r0, pltpu.roll(r1, 64, 1))
            odd = jnp.where(half, pltpu.roll(r0, 64, 1), r1)
            at = ((2 * g) * 8 + h) * 16
            ex_ref[at:at + 16, :] = even.astype(BF16)
            at = ((2 * g + 1) * 8 + h) * 16
            ex_ref[at:at + 16, :] = odd.astype(BF16)


def order_weights(w_ref, owner_ref, panel, wf, w2_ref):
    wf[...] = w_ref[...].astype(F32)
    same = jnp.where(owner_ref[...] == panel, 1.0, 0.0)
    heavy = jnp.zeros((1, 1), F32)
    for block in range(1, 8):
        count = jnp.sum(jnp.sum(same[block * 8:block * 8 + 8], axis=0, keepdims=True), axis=1, keepdims=True)
        heavy = heavy + jnp.where(count > 28.0, float(block), 0.0)
    heavy = heavy.astype(I32)
    slot_lane = iota((1, 512), 1)
    relay, quant, slot = slot_lane >> 6, (slot_lane >> 4) & 3, slot_lane & 15
    panel_at = jnp.where(slot < 12, 12 * relay + jnp.where(relay > heavy, 32, 0) + slot,
                         12 * heavy + 4 * relay + slot)
    mover = hit(iota((512, 512), 0) == quant * 128 + panel_at)
    for k in range(4):
        rows = jnp.concatenate([wf[pl.ds(k * 4 + q, 128, stride=16), :].astype(BF16) for q in range(4)], axis=1)
        w2_ref[k * 128:k * 128 + 128, :] = dot(rows, mover, NN).astype(BF16)


def fill_messages(x, base_in, ex_in, msg):
    low = iota((8, 128), 0) < 4
    lane = iota((8, 128), 1)
    sums = []
    for px in range(NX):
        first = lax.rem(px + NX - x, NX) * NB
        total = ex_in[first].astype(F32)
        for pb in range(1, NB):
            total = total + ex_in[first + pb].astype(F32)
        sums.append(total)
    quants = []
    for v in range(2):
        rows = slice(v * 8, v * 8 + 8)
        e01, o01 = mix_pair(sums[0][rows], sums[1][rows], low)
        e23, o23 = mix_pair(sums[2][rows], sums[3][rows], low)
        quants += [(e01, e23), (o01, o23)]
    bases = [base_in[lax.rem(px + NX - x, NX)].astype(F32) for px in range(NX)]
    masks = [((lane & 63) >= 16 * q + 12) & ((lane & 63) < 16 * q + 16) for q in range(4)]
    for v in range(8):
        rows = slice(v * 8, v * 8 + 8)
        e01, o01 = mix_pair(bases[0][rows], bases[1][rows], low)
        e23, o23 = mix_pair(bases[2][rows], bases[3][rows], low)
        for pz, halves in ((2 * v, (e01, e23)), (2 * v + 1, (o01, o23))):
            done = []
            for h in range(2):
                value = halves[h]
                for q in range(4):
                    shift = (16 * q + 12 - 4 * pz) % 128
                    value = jnp.where(masks[q], pltpu.roll(quants[q][h], shift, 1), value)
                done.append(value)
            msg[pz] = jnp.concatenate(done, axis=0).astype(BF16)


def kernel(donor_hbm, elem_hbm, coord_hbm, owner_hbm, w_hbm, off_ref, out_ref,
           donor, elem_ref, coord_ref, owner_ref, weights, table, hot, src, wf, w2, base_out, ex_out,
           base_in, ex_in, msg, held, wide, part_b, part_in, line, line_in,
           base_s, base_r, ex_s, ex_r, z_s, z_r, o_s, o_r, px_s, px_r, pz_s, pz_r, own_sem):
    panel = lax.axis_index("panel")
    b = lax.axis_index("obs")
    x = lax.div(panel, NZ)
    z = lax.rem(panel, NZ)
    y = lax.div(b, 2)
    core = lax.rem(b, 2)
    xs = [lax.rem(x + i, NX) for i in range(NX)]
    zs = [lax.rem(z + i, NZ) for i in range(NZ)]
    bs = [lax.rem(y + i // 2, 4) * 2 + (core if i % 2 == 0 else 1 - core) for i in range(NB)]

    def at(px, pz, pb):
        return {"panel": px * NZ + pz, "obs": pb}

    def remote(src_ref, dst_ref, send, recv, device):
        return pltpu.make_async_remote_copy(
            src_ref=src_ref, dst_ref=dst_ref, send_sem=send, recv_sem=recv,
            device_id=device, device_id_type=MESH)

    loads = [
        pltpu.make_async_copy(source, target, own_sem.at[i])
        for i, (source, target) in enumerate((
            (coord_hbm, coord_ref), (elem_hbm, elem_ref), (owner_hbm, owner_ref), (donor_hbm, donor),
            (w_hbm, weights)))
    ]
    for load in loads:
        load.start()
    barrier = pltpu.get_barrier_semaphore()

    def greet(i):
        slot = lax.rem(x * NB + b + i, NX * NB)
        pl.semaphore_signal(barrier, inc=1, device_id=at(lax.div(slot, NB), z, lax.rem(slot, NB)),
                            device_id_type=MESH)

    for i in Z_FAR:
        pl.semaphore_signal(barrier, inc=1, device_id=at(x, zs[i], b), device_id_type=MESH)
    loads[0].wait()
    fill_table(coord_ref, table, greet)
    loads[1].wait()
    loads[2].wait()
    hot[...] = hit(iota((128, 1024), 0) == elem_ref[...] - b * 128)
    own = flat_row(owner_ref[pl.ds(pl.multiple_of(b * 8, 8), 8), :])
    rank = rank_points(own)
    loads[3].wait()
    fill_sources(donor, hot, table, src)
    sources = jnp.concatenate([src[tile] for tile in range(8)], axis=1).astype(BF16).astype(F32)
    group_extra(sources, own, rank, ex_out)
    pl.semaphore_wait(barrier, 46)

    def ex_copy(i, j):
        px, pb = xs[i], bs[j]
        back = ((NX - i) % NX) * NB + BACK[j]
        return remote(ex_out.at[pl.ds(pl.multiple_of((px * NB + pb) * 16, 16), 16)], ex_in.at[back],
                      ex_s.at[back], ex_r.at[back], at(px, z, pb))

    def base_copy(i):
        back = (NX - i) % NX
        return remote(base_out.at[pl.ds(pl.multiple_of(xs[i] * 64, 64), 64)], base_in.at[back],
                      base_s.at[back], base_r.at[back], at(xs[i], z, b))

    around = [(i, j) for i in (2, 1, 3, 0) for j in OBS_FAR if i or j]
    for i, j in around:
        ex_copy(i, j).start()
    group_base(sources, own, rank, base_out)
    for i in (2, 1, 3):
        base_copy(i).start()
    own_base = pltpu.make_async_copy(base_out.at[pl.ds(pl.multiple_of(x * 64, 64), 64)], base_in.at[0], own_sem.at[0])
    own_ex = pltpu.make_async_copy(ex_out.at[pl.ds(pl.multiple_of((x * NB + b) * 16, 16), 16)], ex_in.at[0],
                                   own_sem.at[1])
    own_base.start()
    own_ex.start()
    loads[4].wait()
    wide[:, 0:FRONT, :] = jnp.zeros((4, FRONT, 128), F32)
    order_weights(weights, owner_ref, panel, wf, w2)
    own_base.wait()
    own_ex.wait()
    for i, j in around[::-1]:
        ex_copy(i, j).wait_recv()
    for i in (1, 3, 2):
        base_copy(i).wait_recv()
    fill_messages(x, base_in, ex_in, msg)

    def z_copy(i):
        pz = zs[NZ - AWAY[i]]
        return remote(msg.at[pz], held.at[b, pl.ds(i * 16, 16)], z_s.at[i], z_r.at[i], at(x, pz, b))

    for i in range(NZ - 1, 0, -1):
        z_copy(i).start()
    own_z = pltpu.make_async_copy(msg.at[z], held.at[b, pl.ds(0, 16)], own_sem.at[0])
    own_z.start()
    own_z.wait()

    def o_copy(g, source, j, place):
        rows = pl.ds(*GROUPS[g])
        return remote(held.at[source, rows], held.at[source, rows], o_s.at[g * NB + place], o_r.at[g * NB + place],
                      at(x, z, bs[j]))

    def own_out(g, j):
        return o_copy(g, b, j, BACK[j])

    def pass_on(g, j):
        return o_copy(g, bs[j], 1, j + 1)

    begin = 1
    for g in range(3):
        for i in range(begin, GROUP_ENDS[g]):
            z_copy(i).wait_recv()
        begin = GROUP_ENDS[g]
        for j in ((4, 2, 6, 1) if g < 2 else (5, 4, 3, 7, 2, 6, 1)):
            own_out(g, j).start()
    for g in range(2):
        for j in (2, 6, 4):
            own_out(g, BACK[j]).wait_recv()
            pass_on(g, j).start()
    for j in range(1, NB):
        own_out(2, BACK[j]).wait_recv()
    for g in range(2):
        own_out(g, 1).wait_recv()
        for j in (2, 6, 4):
            pass_on(g, j).wait_recv()

    low_wide = iota((8, 512), 0) < 4
    halves = []
    for side in range(2):
        cols = slice(side * 64, side * 64 + 64)
        left = jnp.concatenate([held[pb][:, cols] for pb in range(NB)], axis=1)
        halves.append(dot(left, w2[...], NT))
    for i in range(NZ):
        time = FRONT + 8 * zs[AWAY[i]]
        for xp in range(2):
            rows = slice(i * 16 + xp * 8, i * 16 + xp * 8 + 8)
            pair = mix_pair(halves[0][rows], halves[1][rows], low_wide)
            for side in range(2):
                start = pl.multiple_of(time + 128 * (2 * xp + side), 8)
                for k in range(4):
                    wide[k, pl.ds(start, 8), :] = pair[side][:, k * 128:k * 128 + 128]
    delay = off_ref[0, 0]

    def block(px):
        start = FRONT - delay + px * 128
        total = wide[0, pl.ds(start, 128), :]
        for k in range(1, 4):
            total = total + wide[k, pl.ds(start - k, 128), :]
        return total

    def px_copy(i):
        px = xs[NX - i]
        return remote(part_b.at[i], part_in.at[i], px_s.at[i], px_r.at[i], at(px, z, b))

    for i in (2, 1, 3):
        part_b[i] = block(xs[NX - i]).astype(BF16)
        px_copy(i).start()
    acc = block(x)
    for i in (1, 3, 2):
        px_copy(i).wait_recv()
        acc = acc + part_in[i].astype(F32)
    line[...] = acc

    def pz_copy(i):
        pz = zs[NZ - AWAY[i]]
        return remote(line.at[pl.ds(pl.multiple_of(pz * 8, 8), 8)], line_in.at[i], pz_s.at[i], pz_r.at[i],
                      at(x, pz, b))

    for i in range(NZ - 1, 0, -1):
        pz_copy(i).start()

    for i, j in around:
        ex_copy(i, j).wait_send()
    for i in range(1, NX):
        base_copy(i).wait_send()
        px_copy(i).wait_send()
    for i in range(1, NZ):
        z_copy(i).wait_send()
    for g in range(2):
        for j in (4, 2, 6, 1):
            own_out(g, j).wait_send()
        for j in (2, 6, 4):
            pass_on(g, j).wait_send()
    for j in range(1, NB):
        own_out(2, j).wait_send()
    for i in range(1, NZ):
        pz_copy(i).wait_send()

    acc = line[pl.ds(pl.multiple_of(z * 8, 8), 8), :]
    for i in range(1, NZ):
        pz_copy(i).wait_recv()
        acc = acc + line_in[i]
    out_ref[...] = acc


def body(donor, donor_elem, local_coords, owner, weights, offsets):
    hbm = pl.BlockSpec(memory_space=pltpu.HBM)
    dma = pltpu.SemaphoreType.DMA
    return pl.pallas_call(
        kernel,
        out_shape=jax.ShapeDtypeStruct((8, 128), F32),
        in_specs=[hbm] * 5 + [pl.BlockSpec(memory_space=pltpu.SMEM)],
        out_specs=pl.BlockSpec(memory_space=pltpu.VMEM),
        scratch_shapes=[
            pltpu.VMEM((4000, 128), BF16),
            pltpu.VMEM((1, 1024), I32),
            pltpu.VMEM((3, 1024), F32),
            pltpu.VMEM((64, 128), I32),
            pltpu.VMEM((2048, 128), BF16),
            pltpu.VMEM((1000, 1024), F32),
            pltpu.VMEM((128, 1024), BF16),
            pltpu.VMEM((8, 32, 128), F32),
            pltpu.VMEM((2048, 128), F32),
            pltpu.VMEM((512, 512), BF16),
            pltpu.VMEM((256, 128), BF16),
            pltpu.VMEM((512, 128), BF16),
            pltpu.VMEM((NX, 64, 128), BF16),
            pltpu.VMEM((NX * NB, 16, 128), BF16),
            pltpu.VMEM((NZ, 16, 128), BF16),
            pltpu.VMEM((NB, 256, 128), BF16),
            pltpu.VMEM((4, FRONT + TW, 128), F32),
            pltpu.VMEM((NX, 128, 128), BF16),
            pltpu.VMEM((NX, 128, 128), BF16),
            pltpu.VMEM((128, 128), F32),
            pltpu.VMEM((NZ, 8, 128), F32),
            dma((NX,)), dma((NX,)), dma((32,)), dma((32,)), dma((NZ,)), dma((NZ,)),
            dma((3 * NB,)), dma((3 * NB,)), dma((NX,)), dma((NX,)), dma((NZ,)), dma((NZ,)), dma((5,)),
        ],
        compiler_params=pltpu.CompilerParams(
            collective_id=0, has_side_effects=True, vmem_limit_bytes=60 * 2**20),
    )(
        donor.reshape(4000, 128),
        donor_elem.reshape(1, 1024),
        local_coords,
        owner.reshape(64, 128),
        weights.reshape(2048, 128),
        offsets,
    )


def solution(mesh):
    return jax.shard_map(
        body,
        mesh=mesh,
        in_specs=(
            P("panel", None, None, "obs"),
            P("obs"),
            P(None, "obs"),
            P(),
            P("obs", None, None, "panel"),
            P("obs", "panel"),
        ),
        out_specs=P("panel", "obs"),
        check_vma=False,
    )
```

```python
import jax
import jax.numpy as jnp
from jax import lax
from jax.experimental import pallas as pl
from jax.experimental.pallas import tpu as pltpu
from jax.sharding import PartitionSpec as P

F32 = jnp.float32
BF16 = jnp.bfloat16
I32 = jnp.int32
SPOTS = (-1.0, -0.5, 0.0, 0.5, 1.0)
NX = 4
NZ = 16
NB = 8
FRONT = 264
TW = 512
NT = (((1,), (1,)), ((), ()))
NN = (((1,), (0,)), ((), ()))
MESH = pl.DeviceIdType.MESH
GROUPS = ((0, 112), (112, 96), (208, 48))
GROUP_ENDS = (7, 13, 16)
AWAY = (0, 1, 15, 2, 14, 3, 13, 4, 12, 5, 11, 6, 10, 7, 9, 8)
Z_FAR = AWAY[:0:-1]
OBS_FAR = (5, 4, 3, 7, 2, 6, 1, 0)
BACK = (0, 1, 6, 7, 4, 5, 2, 3)


def iota(shape, axis):
    return lax.broadcasted_iota(I32, shape, axis)


def dot(a, b, dims):
    return lax.dot_general(a, b, dims, preferred_element_type=F32)


def hit(cond):
    return jnp.where(cond, 1.0, 0.0).astype(BF16)


def flat_row(tiles):
    return jnp.concatenate([tiles[t:t + 1] for t in range(8)], axis=1)


def mix_pair(a, b, low):
    return jnp.where(low, a, pltpu.roll(b, 4, 0)), jnp.where(low, pltpu.roll(a, 4, 0), b)


def fill_table(coord_ref, table, greet):
    def table_step(tile):
        lanes = pl.ds(pl.multiple_of(tile * 128, 128), 128)
        factors = []
        for direction in range(3):
            x = jnp.broadcast_to(coord_ref[direction:direction + 1, lanes], (8, 128))
            column = []
            for one in range(5):
                value = None
                for two in range(5):
                    if two != one:
                        term = (x - SPOTS[two]) * (1.0 / (SPOTS[one] - SPOTS[two]))
                        value = term if value is None else value * term
                column.append(value)
            factors.append(column)
        low = iota((8, 128), 0) < 4
        pairs = [[fa * fb for fb in factors[1]] for fa in factors[0]]
        nodes = [pairs[n // 25][(n // 5) % 5] * factors[2][n % 5] for n in range(125)]
        for j in range(125):
            table[8 * j:8 * j + 8, lanes] = jnp.where(low, nodes[(2 * j) % 125], nodes[(2 * j + 1) % 125])

    def table_loop(tile, carry):
        for k in range(4):
            greet(4 * tile + k)
        table_step(tile)
        return carry

    lax.fori_loop(1, 8, table_loop, 0)
    for k in range(1, 4):
        greet(k)
    table_step(0)


def fill_sources(donor, hot, table, src, ready):
    edges = (0, 62, 63, 125, 187, 188, 250)
    for part in range(2):
        ready(part)
        sums = [None] * 6
        for piece in range(5):
            row = part * 2000 + piece * 400
            picked = dot(donor[row:row + 400, :], hot[...], NN)
            for k in range(6):
                begin, end = max(edges[k], piece * 50), min(edges[k + 1], piece * 50 + 50)
                if begin < end:
                    at = 8 * (begin - piece * 50)
                    size = 8 * (end - begin)
                    prod = picked[at:at + size] * table[8 * (begin % 125):8 * (begin % 125) + size, :]
                    value = jnp.sum(prod.reshape(end - begin, 8, 1024), axis=0)
                    sums[k] = value if sums[k] is None else sums[k] + value
        for half in range(2):
            first, mid, last = sums[3 * half:3 * half + 3]
            step = 16 * part + 2 * half
            even = first[:4] + first[4:] + mid[:4]
            odd = last[:4] + last[4:] + mid[4:]
            for tile in range(8):
                cols = slice(tile * 128, tile * 128 + 128)
                src[tile, pl.ds(step, 4, stride=4), :] = even[:, cols]
                src[tile, pl.ds(step + 1, 4, stride=4), :] = odd[:, cols]


def rank_points(own):
    member = iota((64, 1024), 0) == own
    member_f = jnp.where(member, 1.0, 0.0)
    member_b = member_f.astype(BF16)
    upper = hit(iota((128, 128), 0) < iota((128, 128), 1))
    ones = jnp.ones((128, 128), BF16)
    carry = jnp.zeros((64, 128), F32)
    ranks = []
    for tile in range(8):
        cols = slice(tile * 128, tile * 128 + 128)
        below = dot(member_b[:, cols], upper, NN) + carry
        ranks.append(jnp.sum(member_f[:, cols] * below, axis=0, keepdims=True))
        carry = carry + dot(member_b[:, cols], ones, NN)
    return jnp.concatenate(ranks, axis=1).astype(I32)


def fill_places(own, rank, place_base, place_extra):
    spot = jnp.where(rank < 12, (own & 7) * 16 + rank, -1)
    place_base[...] = hit(iota((128, 1024), 0) == spot)
    spot = jnp.where(rank >= 12, ((own >> 4) & 1) * 64 + (own & 15) * 4 + (rank & 3), -1)
    place_extra[...] = hit(iota((128, 1024), 0) == spot)


def group_base(sources, own, place, base_ref):
    group = own >> 3
    left = jnp.concatenate([jnp.where(group == g, sources, 0.0).astype(BF16) for g in range(8)], axis=0)
    grouped = dot(left, place[...], NT)
    row = iota((32, 128), 0)
    lane = iota((32, 128), 1)
    for g in range(8):
        x = grouped[g * 32:g * 32 + 32]
        for k in range(3):
            r, l = 4 << k, 16 << k
            rbit, lbit = (row >> (2 + k)) & 1, (lane >> (4 + k)) & 1
            up = pltpu.roll(pltpu.roll(x, 32 - r, 0), l, 1)
            down = pltpu.roll(pltpu.roll(x, r, 0), 128 - l, 1)
            x = jnp.where(rbit == lbit, x, jnp.where(rbit == 0, up, down))
        base_ref[g * 32:g * 32 + 32, :] = x.astype(BF16)


def group_extra(sources, own, rank, place, ex_ref):
    group = (own >> 5) * 8 + ((rank - 12) >> 2)
    half = iota((16, 128), 1) < 64
    for g in range(2):
        left = jnp.concatenate(
            [jnp.where(group == g * 8 + h, sources, 0.0).astype(BF16) for h in range(8)], axis=0)
        more = dot(left, place[...], NT)
        for h in range(8):
            r0, r1 = more[h * 32:h * 32 + 16], more[h * 32 + 16:h * 32 + 32]
            even = jnp.where(half, r0, pltpu.roll(r1, 64, 1))
            odd = jnp.where(half, pltpu.roll(r0, 64, 1), r1)
            at = ((2 * g) * 8 + h) * 16
            ex_ref[at:at + 16, :] = even.astype(BF16)
            at = ((2 * g + 1) * 8 + h) * 16
            ex_ref[at:at + 16, :] = odd.astype(BF16)


def order_weights(w_ref, owner_ref, panel, wf, w2_ref):
    wf[...] = w_ref[...].astype(F32)
    same = jnp.where(owner_ref[...] == panel, 1.0, 0.0)
    heavy = jnp.zeros((1, 1), F32)
    for block in range(1, 8):
        count = jnp.sum(jnp.sum(same[block * 8:block * 8 + 8], axis=0, keepdims=True), axis=1, keepdims=True)
        heavy = heavy + jnp.where(count > 28.0, float(block), 0.0)
    heavy = heavy.astype(I32)
    slot_lane = iota((1, 512), 1)
    relay, quant, slot = slot_lane >> 6, (slot_lane >> 4) & 3, slot_lane & 15
    panel_at = jnp.where(slot < 12, 12 * relay + jnp.where(relay > heavy, 32, 0) + slot,
                         12 * heavy + 4 * relay + slot)
    mover = hit(iota((512, 512), 0) == quant * 128 + panel_at)
    for k in range(4):
        rows = jnp.concatenate([wf[pl.ds(k * 4 + q, 128, stride=16), :].astype(BF16) for q in range(4)], axis=1)
        w2_ref[k * 128:k * 128 + 128, :] = dot(rows, mover, NN).astype(BF16)


def fill_messages(x, base_in, ex_in, msg):
    low = iota((8, 128), 0) < 4
    lane = iota((8, 128), 1)
    sums = []
    for px in range(NX):
        first = lax.rem(px + NX - x, NX) * NB
        total = ex_in[first].astype(F32)
        for pb in range(1, NB):
            total = total + ex_in[first + pb].astype(F32)
        sums.append(total)
    quants = []
    for v in range(2):
        rows = slice(v * 8, v * 8 + 8)
        e01, o01 = mix_pair(sums[0][rows], sums[1][rows], low)
        e23, o23 = mix_pair(sums[2][rows], sums[3][rows], low)
        quants += [(e01, e23), (o01, o23)]
    bases = [base_in[lax.rem(px + NX - x, NX)].astype(F32) for px in range(NX)]
    masks = [((lane & 63) >= 16 * q + 12) & ((lane & 63) < 16 * q + 16) for q in range(4)]
    for v in range(8):
        rows = slice(v * 8, v * 8 + 8)
        e01, o01 = mix_pair(bases[0][rows], bases[1][rows], low)
        e23, o23 = mix_pair(bases[2][rows], bases[3][rows], low)
        for pz, halves in ((2 * v, (e01, e23)), (2 * v + 1, (o01, o23))):
            done = []
            for h in range(2):
                value = halves[h]
                for q in range(4):
                    shift = (16 * q + 12 - 4 * pz) % 128
                    value = jnp.where(masks[q], pltpu.roll(quants[q][h], shift, 1), value)
                done.append(value)
            msg[pz] = jnp.concatenate(done, axis=0).astype(BF16)


def kernel(donor_hbm, elem_hbm, coord_hbm, owner_hbm, w_hbm, off_ref, out_ref,
           donor, elem_ref, coord_ref, owner_ref, weights, place_base, place_extra, table, hot, src, wf, w2, base_out, ex_out,
           base_in, ex_in, msg, held, wide, part_b, part_in, line, line_in,
           base_s, base_r, ex_s, ex_r, z_s, z_r, o_s, o_r, px_s, px_r, pz_s, pz_r, own_sem):
    panel = lax.axis_index("panel")
    b = lax.axis_index("obs")
    x = lax.div(panel, NZ)
    z = lax.rem(panel, NZ)
    y = lax.div(b, 2)
    core = lax.rem(b, 2)
    xs = [lax.rem(x + i, NX) for i in range(NX)]
    zs = [lax.rem(z + i, NZ) for i in range(NZ)]
    bs = [lax.rem(y + i // 2, 4) * 2 + (core if i % 2 == 0 else 1 - core) for i in range(NB)]

    def at(px, pz, pb):
        return {"panel": px * NZ + pz, "obs": pb}

    def remote(src_ref, dst_ref, send, recv, device):
        return pltpu.make_async_remote_copy(
            src_ref=src_ref, dst_ref=dst_ref, send_sem=send, recv_sem=recv,
            device_id=device, device_id_type=MESH)

    loads = [
        pltpu.make_async_copy(source, target, own_sem.at[i])
        for i, (source, target) in enumerate((
            (coord_hbm, coord_ref), (elem_hbm, elem_ref), (owner_hbm, owner_ref),
            (donor_hbm.at[0:2000], donor.at[0:2000]), (donor_hbm.at[2000:4000], donor.at[2000:4000]),
            (w_hbm, weights)))
    ]
    for load in loads:
        load.start()
    barrier = pltpu.get_barrier_semaphore()

    def greet(i):
        slot = lax.rem(x * NB + b + i, NX * NB)
        pl.semaphore_signal(barrier, inc=1, device_id=at(lax.div(slot, NB), z, lax.rem(slot, NB)),
                            device_id_type=MESH)

    for i in Z_FAR:
        pl.semaphore_signal(barrier, inc=1, device_id=at(x, zs[i], b), device_id_type=MESH)
    loads[0].wait()
    fill_table(coord_ref, table, greet)
    loads[1].wait()
    loads[2].wait()
    hot[...] = hit(iota((128, 1024), 0) == elem_ref[...] - b * 128)
    own = flat_row(owner_ref[pl.ds(pl.multiple_of(b * 8, 8), 8), :])
    rank = rank_points(own)
    fill_places(own, rank, place_base, place_extra)
    fill_sources(donor, hot, table, src, lambda part: loads[3 + part].wait())
    sources = jnp.concatenate([src[tile] for tile in range(8)], axis=1).astype(BF16).astype(F32)
    group_extra(sources, own, rank, place_extra, ex_out)
    pl.semaphore_wait(barrier, 46)

    def ex_copy(i, j):
        px, pb = xs[i], bs[j]
        back = ((NX - i) % NX) * NB + BACK[j]
        return remote(ex_out.at[pl.ds(pl.multiple_of((px * NB + pb) * 16, 16), 16)], ex_in.at[back],
                      ex_s.at[back], ex_r.at[back], at(px, z, pb))

    def base_copy(i):
        back = (NX - i) % NX
        return remote(base_out.at[pl.ds(pl.multiple_of(xs[i] * 64, 64), 64)], base_in.at[back],
                      base_s.at[back], base_r.at[back], at(xs[i], z, b))

    around = [(i, j) for i in (2, 1, 3, 0) for j in OBS_FAR if i or j]
    for i, j in around:
        ex_copy(i, j).start()
    group_base(sources, own, place_base, base_out)
    for i in (2, 1, 3):
        base_copy(i).start()
    own_base = pltpu.make_async_copy(base_out.at[pl.ds(pl.multiple_of(x * 64, 64), 64)], base_in.at[0], own_sem.at[0])
    own_ex = pltpu.make_async_copy(ex_out.at[pl.ds(pl.multiple_of((x * NB + b) * 16, 16), 16)], ex_in.at[0],
                                   own_sem.at[1])
    own_base.start()
    own_ex.start()
    loads[5].wait()
    wide[:, 0:FRONT, :] = jnp.zeros((4, FRONT, 128), F32)
    order_weights(weights, owner_ref, panel, wf, w2)
    own_base.wait()
    own_ex.wait()
    for i, j in around[::-1]:
        ex_copy(i, j).wait_recv()
    for i in (1, 3, 2):
        base_copy(i).wait_recv()
    fill_messages(x, base_in, ex_in, msg)

    def z_copy(i):
        pz = zs[NZ - AWAY[i]]
        return remote(msg.at[pz], held.at[b, pl.ds(i * 16, 16)], z_s.at[i], z_r.at[i], at(x, pz, b))

    for i in range(NZ - 1, 0, -1):
        z_copy(i).start()
    own_z = pltpu.make_async_copy(msg.at[z], held.at[b, pl.ds(0, 16)], own_sem.at[0])
    own_z.start()
    own_z.wait()

    def o_copy(g, source, j, place):
        rows = pl.ds(*GROUPS[g])
        return remote(held.at[source, rows], held.at[source, rows], o_s.at[g * NB + place], o_r.at[g * NB + place],
                      at(x, z, bs[j]))

    def own_out(g, j):
        return o_copy(g, b, j, BACK[j])

    def pass_on(g, j):
        return o_copy(g, bs[j], 1, j + 1)

    begin = 1
    for g in range(3):
        for i in range(begin, GROUP_ENDS[g]):
            z_copy(i).wait_recv()
        begin = GROUP_ENDS[g]
        for j in ((4, 2, 6, 1) if g < 2 else (5, 4, 3, 7, 2, 6, 1)):
            own_out(g, j).start()
    for g in range(2):
        for j in (2, 6, 4):
            own_out(g, BACK[j]).wait_recv()
            pass_on(g, j).start()
    for j in range(1, NB):
        own_out(2, BACK[j]).wait_recv()
    for g in range(2):
        own_out(g, 1).wait_recv()
        for j in (2, 6, 4):
            pass_on(g, j).wait_recv()

    low_wide = iota((8, 512), 0) < 4
    halves = []
    for side in range(2):
        cols = slice(side * 64, side * 64 + 64)
        left = jnp.concatenate([held[pb][:, cols] for pb in range(NB)], axis=1)
        halves.append(dot(left, w2[...], NT))
    for i in range(NZ):
        time = FRONT + 8 * zs[AWAY[i]]
        for xp in range(2):
            rows = slice(i * 16 + xp * 8, i * 16 + xp * 8 + 8)
            pair = mix_pair(halves[0][rows], halves[1][rows], low_wide)
            for side in range(2):
                start = pl.multiple_of(time + 128 * (2 * xp + side), 8)
                for k in range(4):
                    wide[k, pl.ds(start, 8), :] = pair[side][:, k * 128:k * 128 + 128]
    delay = off_ref[0, 0]

    def block(px):
        start = FRONT - delay + px * 128
        total = wide[0, pl.ds(start, 128), :]
        for k in range(1, 4):
            total = total + wide[k, pl.ds(start - k, 128), :]
        return total

    def px_copy(i):
        px = xs[NX - i]
        return remote(part_b.at[i], part_in.at[i], px_s.at[i], px_r.at[i], at(px, z, b))

    for i in (2, 1, 3):
        part_b[i] = block(xs[NX - i]).astype(BF16)
        px_copy(i).start()
    acc = block(x)
    for i in (1, 3, 2):
        px_copy(i).wait_recv()
        acc = acc + part_in[i].astype(F32)
    line[...] = acc

    def pz_copy(i):
        pz = zs[NZ - AWAY[i]]
        return remote(line.at[pl.ds(pl.multiple_of(pz * 8, 8), 8)], line_in.at[i], pz_s.at[i], pz_r.at[i],
                      at(x, pz, b))

    for i in range(NZ - 1, 0, -1):
        pz_copy(i).start()

    for i, j in around:
        ex_copy(i, j).wait_send()
    for i in range(1, NX):
        base_copy(i).wait_send()
        px_copy(i).wait_send()
    for i in range(1, NZ):
        z_copy(i).wait_send()
    for g in range(2):
        for j in (4, 2, 6, 1):
            own_out(g, j).wait_send()
        for j in (2, 6, 4):
            pass_on(g, j).wait_send()
    for j in range(1, NB):
        own_out(2, j).wait_send()
    for i in range(1, NZ):
        pz_copy(i).wait_send()

    acc = line[pl.ds(pl.multiple_of(z * 8, 8), 8), :]
    for i in range(1, NZ):
        pz_copy(i).wait_recv()
        acc = acc + line_in[i]
    out_ref[...] = acc


def body(donor, donor_elem, local_coords, owner, weights, offsets):
    hbm = pl.BlockSpec(memory_space=pltpu.HBM)
    dma = pltpu.SemaphoreType.DMA
    return pl.pallas_call(
        kernel,
        out_shape=jax.ShapeDtypeStruct((8, 128), F32),
        in_specs=[hbm] * 5 + [pl.BlockSpec(memory_space=pltpu.SMEM)],
        out_specs=pl.BlockSpec(memory_space=pltpu.VMEM),
        scratch_shapes=[
            pltpu.VMEM((4000, 128), BF16),
            pltpu.VMEM((1, 1024), I32),
            pltpu.VMEM((3, 1024), F32),
            pltpu.VMEM((64, 128), I32),
            pltpu.VMEM((2048, 128), BF16),
            pltpu.VMEM((128, 1024), BF16),
            pltpu.VMEM((128, 1024), BF16),
            pltpu.VMEM((1000, 1024), F32),
            pltpu.VMEM((128, 1024), BF16),
            pltpu.VMEM((8, 32, 128), F32),
            pltpu.VMEM((2048, 128), F32),
            pltpu.VMEM((512, 512), BF16),
            pltpu.VMEM((256, 128), BF16),
            pltpu.VMEM((512, 128), BF16),
            pltpu.VMEM((NX, 64, 128), BF16),
            pltpu.VMEM((NX * NB, 16, 128), BF16),
            pltpu.VMEM((NZ, 16, 128), BF16),
            pltpu.VMEM((NB, 256, 128), BF16),
            pltpu.VMEM((4, FRONT + TW, 128), F32),
            pltpu.VMEM((NX, 128, 128), BF16),
            pltpu.VMEM((NX, 128, 128), BF16),
            pltpu.VMEM((128, 128), F32),
            pltpu.VMEM((NZ, 8, 128), F32),
            dma((NX,)), dma((NX,)), dma((32,)), dma((32,)), dma((NZ,)), dma((NZ,)),
            dma((3 * NB,)), dma((3 * NB,)), dma((NX,)), dma((NX,)), dma((NZ,)), dma((NZ,)), dma((6,)),
        ],
        compiler_params=pltpu.CompilerParams(
            collective_id=0, has_side_effects=True, vmem_limit_bytes=55228 * 1024),
    )(
        donor.reshape(4000, 128),
        donor_elem.reshape(1, 1024),
        local_coords,
        owner.reshape(64, 128),
        weights.reshape(2048, 128),
        offsets,
    )


def solution(mesh):
    return jax.shard_map(
        body,
        mesh=mesh,
        in_specs=(
            P("panel", None, None, "obs"),
            P("obs"),
            P(None, "obs"),
            P(),
            P("obs", None, None, "panel"),
            P("obs", "panel"),
        ),
        out_specs=P("panel", "obs"),
        check_vma=False,
    )
```

```python
import jax
import jax.numpy as jnp
from jax import lax
from jax.experimental import pallas as pl
from jax.experimental.pallas import tpu as pltpu
from jax.sharding import PartitionSpec as P

F32 = jnp.float32
BF16 = jnp.bfloat16
I32 = jnp.int32
SPOTS = (-1.0, -0.5, 0.0, 0.5, 1.0)
NX = 4
NZ = 16
NB = 8
FRONT = 264
TW = 512
NT = (((1,), (1,)), ((), ()))
NN = (((1,), (0,)), ((), ()))
MESH = pl.DeviceIdType.MESH
GROUPS = ((0, 112), (112, 96), (208, 48))
GROUP_ENDS = (7, 13, 16)
AWAY = (0, 1, 15, 2, 14, 3, 13, 4, 12, 5, 11, 6, 10, 7, 9, 8)
Z_FAR = AWAY[:0:-1]
OBS_FAR = (5, 4, 3, 7, 2, 6, 1, 0)
BACK = (0, 1, 6, 7, 4, 5, 2, 3)
BASE_S, BASE_R, EX_S, EX_R, Z_S, Z_R, Y_R, O_S, O_R, PX_S, PX_R, PZ_S, PZ_R, OWN = (
    0, 1, 2, 3, 4, 5, 8, 10, 13, 16, 17, 18, 19, 20)


def iota(shape, axis):
    return lax.broadcasted_iota(I32, shape, axis)


def dot(a, b, dims):
    return lax.dot_general(a, b, dims, preferred_element_type=F32)


def hit(cond):
    return jnp.where(cond, 1.0, 0.0).astype(BF16)


def flat_row(tiles):
    return jnp.concatenate([tiles[t:t + 1] for t in range(8)], axis=1)


def mix_pair(a, b, low):
    return jnp.where(low, a, pltpu.roll(b, 4, 0)), jnp.where(low, pltpu.roll(a, 4, 0), b)


def fill_table(coord_ref, table, greet):
    def table_step(tile):
        lanes = pl.ds(pl.multiple_of(tile * 128, 128), 128)
        factors = []
        for direction in range(3):
            x = jnp.broadcast_to(coord_ref[direction:direction + 1, lanes], (8, 128))
            column = []
            for one in range(5):
                value = None
                for two in range(5):
                    if two != one:
                        term = (x - SPOTS[two]) * (1.0 / (SPOTS[one] - SPOTS[two]))
                        value = term if value is None else value * term
                column.append(value)
            factors.append(column)
        low = iota((8, 128), 0) < 4
        pairs = [[fa * fb for fb in factors[1]] for fa in factors[0]]
        nodes = [pairs[n // 25][(n // 5) % 5] * factors[2][n % 5] for n in range(125)]
        for j in range(125):
            table[8 * j:8 * j + 8, lanes] = jnp.where(low, nodes[(2 * j) % 125], nodes[(2 * j + 1) % 125])

    def table_loop(tile, carry):
        for k in range(4):
            greet(4 * tile + k)
        table_step(tile)
        return carry

    lax.fori_loop(1, 8, table_loop, 0)
    for k in range(1, 4):
        greet(k)
    table_step(0)


def fill_sources(donor, hot, table, src, ready):
    edges = (0, 62, 63, 125, 187, 188, 250)
    for part in range(2):
        ready(part)
        sums = [None] * 6
        for piece in range(5):
            row = part * 2000 + piece * 400
            picked = dot(donor[row:row + 400, :], hot[...], NN)
            for k in range(6):
                begin, end = max(edges[k], piece * 50), min(edges[k + 1], piece * 50 + 50)
                if begin < end:
                    at = 8 * (begin - piece * 50)
                    size = 8 * (end - begin)
                    prod = picked[at:at + size] * table[8 * (begin % 125):8 * (begin % 125) + size, :]
                    value = jnp.sum(prod.reshape(end - begin, 8, 1024), axis=0)
                    sums[k] = value if sums[k] is None else sums[k] + value
        for half in range(2):
            first, mid, last = sums[3 * half:3 * half + 3]
            step = 16 * part + 2 * half
            even = first[:4] + first[4:] + mid[:4]
            odd = last[:4] + last[4:] + mid[4:]
            for tile in range(8):
                cols = slice(tile * 128, tile * 128 + 128)
                src[tile, pl.ds(step, 4, stride=4), :] = even[:, cols]
                src[tile, pl.ds(step + 1, 4, stride=4), :] = odd[:, cols]


def rank_points(own):
    member = iota((64, 1024), 0) == own
    member_f = jnp.where(member, 1.0, 0.0)
    member_b = member_f.astype(BF16)
    upper = hit(iota((128, 128), 0) < iota((128, 128), 1))
    ones = jnp.ones((128, 128), BF16)
    carry = jnp.zeros((64, 128), F32)
    ranks = []
    for tile in range(8):
        cols = slice(tile * 128, tile * 128 + 128)
        below = dot(member_b[:, cols], upper, NN) + carry
        ranks.append(jnp.sum(member_f[:, cols] * below, axis=0, keepdims=True))
        carry = carry + dot(member_b[:, cols], ones, NN)
    return jnp.concatenate(ranks, axis=1).astype(I32)


def fill_places(own, rank, place_base, place_extra):
    spot = jnp.where(rank < 12, (own & 7) * 16 + rank, -1)
    place_base[...] = hit(iota((128, 1024), 0) == spot)
    spot = jnp.where(rank >= 12, ((own >> 4) & 1) * 64 + (own & 15) * 4 + (rank & 3), -1)
    place_extra[...] = hit(iota((128, 1024), 0) == spot)


def group_base(sources, own, place, base_ref):
    group = own >> 3
    left = jnp.concatenate([jnp.where(group == g, sources, 0.0).astype(BF16) for g in range(8)], axis=0)
    grouped = dot(left, place[...], NT)
    row = iota((32, 128), 0)
    lane = iota((32, 128), 1)
    for g in range(8):
        x = grouped[g * 32:g * 32 + 32]
        for k in range(3):
            r, l = 4 << k, 16 << k
            rbit, lbit = (row >> (2 + k)) & 1, (lane >> (4 + k)) & 1
            up = pltpu.roll(pltpu.roll(x, 32 - r, 0), l, 1)
            down = pltpu.roll(pltpu.roll(x, r, 0), 128 - l, 1)
            x = jnp.where(rbit == lbit, x, jnp.where(rbit == 0, up, down))
        base_ref[g * 32:g * 32 + 32, :] = x.astype(BF16)


def group_extra(sources, own, rank, place, ex_ref):
    group = (own >> 5) * 8 + ((rank - 12) >> 2)
    half = iota((16, 128), 1) < 64
    for g in range(2):
        left = jnp.concatenate(
            [jnp.where(group == g * 8 + h, sources, 0.0).astype(BF16) for h in range(8)], axis=0)
        more = dot(left, place[...], NT)
        for h in range(8):
            r0, r1 = more[h * 32:h * 32 + 16], more[h * 32 + 16:h * 32 + 32]
            even = jnp.where(half, r0, pltpu.roll(r1, 64, 1))
            odd = jnp.where(half, pltpu.roll(r0, 64, 1), r1)
            at = ((2 * g) * 8 + h) * 16
            ex_ref[at:at + 16, :] = even.astype(BF16)
            at = ((2 * g + 1) * 8 + h) * 16
            ex_ref[at:at + 16, :] = odd.astype(BF16)


def order_weights(w_ref, owner_ref, panel, wf, w2_ref):
    wf[...] = w_ref[...].astype(F32)
    same = jnp.where(owner_ref[...] == panel, 1.0, 0.0)
    heavy = jnp.zeros((1, 1), F32)
    for block in range(1, 8):
        count = jnp.sum(jnp.sum(same[block * 8:block * 8 + 8], axis=0, keepdims=True), axis=1, keepdims=True)
        heavy = heavy + jnp.where(count > 28.0, float(block), 0.0)
    heavy = heavy.astype(I32)
    slot_lane = iota((1, 512), 1)
    relay, quant, slot = slot_lane >> 6, (slot_lane >> 4) & 3, slot_lane & 15
    panel_at = jnp.where(slot < 12, 12 * relay + jnp.where(relay > heavy, 32, 0) + slot,
                         12 * heavy + 4 * relay + slot)
    mover = hit(iota((512, 512), 0) == quant * 128 + panel_at)
    for k in range(4):
        rows = jnp.concatenate([wf[pl.ds(k * 4 + q, 128, stride=16), :].astype(BF16) for q in range(4)], axis=1)
        w2_ref[k * 128:k * 128 + 128, :] = dot(rows, mover, NN).astype(BF16)


def fill_messages(x, base_in, ex_in, msg):
    low = iota((8, 128), 0) < 4
    lane = iota((8, 128), 1)
    sums = []
    for px in range(NX):
        first = lax.rem(px + NX - x, NX) * NB
        total = ex_in[first].astype(F32)
        for pb in range(1, NB):
            total = total + ex_in[first + pb].astype(F32)
        sums.append(total)
    quants = []
    for v in range(2):
        rows = slice(v * 8, v * 8 + 8)
        e01, o01 = mix_pair(sums[0][rows], sums[1][rows], low)
        e23, o23 = mix_pair(sums[2][rows], sums[3][rows], low)
        quants += [(e01, e23), (o01, o23)]
    bases = [base_in[lax.rem(px + NX - x, NX)].astype(F32) for px in range(NX)]
    masks = [((lane & 63) >= 16 * q + 12) & ((lane & 63) < 16 * q + 16) for q in range(4)]
    for v in range(8):
        rows = slice(v * 8, v * 8 + 8)
        e01, o01 = mix_pair(bases[0][rows], bases[1][rows], low)
        e23, o23 = mix_pair(bases[2][rows], bases[3][rows], low)
        for pz, halves in ((2 * v, (e01, e23)), (2 * v + 1, (o01, o23))):
            done = []
            for h in range(2):
                value = halves[h]
                for q in range(4):
                    shift = (16 * q + 12 - 4 * pz) % 128
                    value = jnp.where(masks[q], pltpu.roll(quants[q][h], shift, 1), value)
                done.append(value)
            msg[pz] = jnp.concatenate(done, axis=0).astype(BF16)


def kernel(donor_hbm, elem_hbm, coord_hbm, owner_hbm, w_hbm, off_ref, out_ref,
           donor, elem_ref, coord_ref, owner_ref, weights, place_base, place_extra, table, hot, src, wf, w2, base_out, ex_out,
           base_in, ex_in, msg, held, wide, part_b, part_in, line, line_in,
           sems):
    panel = lax.axis_index("panel")
    b = lax.axis_index("obs")
    x = lax.div(panel, NZ)
    z = lax.rem(panel, NZ)
    y = lax.div(b, 2)
    core = lax.rem(b, 2)
    xs = [lax.rem(x + i, NX) for i in range(NX)]
    zs = [lax.rem(z + i, NZ) for i in range(NZ)]
    bs = [lax.rem(y + i // 2, 4) * 2 + (core if i % 2 == 0 else 1 - core) for i in range(NB)]

    def at(px, pz, pb):
        return {"panel": px * NZ + pz, "obs": pb}

    def remote(src_ref, dst_ref, send, recv, device):
        return pltpu.make_async_remote_copy(
            src_ref=src_ref, dst_ref=dst_ref, send_sem=sems.at[send], recv_sem=sems.at[recv],
            device_id=device, device_id_type=MESH)

    def settle(ref, which):
        pltpu.make_async_copy(ref, ref, sems.at[which]).wait()

    loads = [
        pltpu.make_async_copy(source, target, sems.at[OWN + i])
        for i, (source, target) in enumerate((
            (coord_hbm, coord_ref), (elem_hbm, elem_ref), (owner_hbm, owner_ref),
            (donor_hbm.at[0:2000], donor.at[0:2000]), (donor_hbm.at[2000:4000], donor.at[2000:4000]),
            (w_hbm, weights)))
    ]
    for load in loads:
        load.start()
    barrier = pltpu.get_barrier_semaphore()

    def greet(i):
        slot = lax.rem(x * NB + b + i, NX * NB)
        pl.semaphore_signal(barrier, inc=1, device_id=at(lax.div(slot, NB), z, lax.rem(slot, NB)),
                            device_id_type=MESH)

    for i in Z_FAR:
        pl.semaphore_signal(barrier, inc=1, device_id=at(x, zs[i], b), device_id_type=MESH)
    loads[0].wait()
    fill_table(coord_ref, table, greet)
    loads[1].wait()
    loads[2].wait()
    hot[...] = hit(iota((128, 1024), 0) == elem_ref[...] - b * 128)
    own = flat_row(owner_ref[pl.ds(pl.multiple_of(b * 8, 8), 8), :])
    rank = rank_points(own)
    fill_places(own, rank, place_base, place_extra)
    fill_sources(donor, hot, table, src, lambda part: loads[3 + part].wait())
    sources = jnp.concatenate([src[tile] for tile in range(8)], axis=1).astype(BF16).astype(F32)
    group_extra(sources, own, rank, place_extra, ex_out)
    pl.semaphore_wait(barrier, 46)

    def ex_copy(i, j):
        px, pb = xs[i], bs[j]
        back = ((NX - i) % NX) * NB + BACK[j]
        return remote(ex_out.at[pl.ds(pl.multiple_of((px * NB + pb) * 16, 16), 16)], ex_in.at[back],
                      EX_S, EX_R, at(px, z, pb))

    def base_copy(i):
        back = (NX - i) % NX
        return remote(base_out.at[pl.ds(pl.multiple_of(xs[i] * 64, 64), 64)], base_in.at[back],
                      BASE_S, BASE_R, at(xs[i], z, b))

    around = [(i, j) for i in (2, 1, 3, 0) for j in OBS_FAR if i or j]
    for i, j in around:
        ex_copy(i, j).start()
    group_base(sources, own, place_base, base_out)
    for i in (2, 1, 3):
        base_copy(i).start()
    own_base = pltpu.make_async_copy(base_out.at[pl.ds(pl.multiple_of(x * 64, 64), 64)], base_in.at[0], sems.at[OWN])
    own_ex = pltpu.make_async_copy(ex_out.at[pl.ds(pl.multiple_of((x * NB + b) * 16, 16), 16)], ex_in.at[0],
                                   sems.at[OWN + 1])
    own_base.start()
    own_ex.start()
    loads[5].wait()
    wide[:, 0:FRONT, :] = jnp.zeros((4, FRONT, 128), F32)
    order_weights(weights, owner_ref, panel, wf, w2)
    own_base.wait()
    own_ex.wait()
    settle(ex_in.at[1:NX * NB], EX_R)
    settle(base_in.at[1:NX], BASE_R)
    fill_messages(x, base_in, ex_in, msg)

    def z_copy(i):
        pz = zs[NZ - AWAY[i]]
        group = sum(i >= end for end in GROUP_ENDS)
        return remote(msg.at[pz], held.at[b, pl.ds(i * 16, 16)], Z_S, Z_R + group, at(x, pz, b))

    for i in range(NZ - 1, 0, -1):
        z_copy(i).start()
    own_z = pltpu.make_async_copy(msg.at[z], held.at[b, pl.ds(0, 16)], sems.at[OWN])
    own_z.start()
    own_z.wait()

    def o_copy(g, source, j, recv):
        rows = pl.ds(*GROUPS[g])
        return remote(held.at[source, rows], held.at[source, rows], O_S + g, recv, at(x, z, bs[j]))

    def pieces(g, n):
        return held.at[0:n, pl.ds(*GROUPS[g])]

    for g in range(3):
        first, size = GROUPS[g]
        skip = 16 if g == 0 else 0
        settle(held.at[b, pl.ds(first + skip, size - skip)], Z_R + g)
        for j in ((4, 2, 6, 1) if g < 2 else (5, 4, 3, 7, 2, 6, 1)):
            o_copy(g, b, j, Y_R + g if g < 2 and j > 1 else O_R + g).start()
    for g in range(2):
        settle(pieces(g, 3), Y_R + g)
        for j in (2, 6, 4):
            o_copy(g, bs[j], 1, O_R + g).start()
    for g in range(3):
        settle(pieces(g, 4 if g < 2 else 7), O_R + g)

    low_wide = iota((8, 512), 0) < 4
    halves = []
    for side in range(2):
        cols = slice(side * 64, side * 64 + 64)
        left = jnp.concatenate([held[pb][:, cols] for pb in range(NB)], axis=1)
        halves.append(dot(left, w2[...], NT))
    for i in range(NZ):
        time = FRONT + 8 * zs[AWAY[i]]
        for xp in range(2):
            rows = slice(i * 16 + xp * 8, i * 16 + xp * 8 + 8)
            pair = mix_pair(halves[0][rows], halves[1][rows], low_wide)
            for side in range(2):
                start = pl.multiple_of(time + 128 * (2 * xp + side), 8)
                for k in range(4):
                    wide[k, pl.ds(start, 8), :] = pair[side][:, k * 128:k * 128 + 128]
    delay = off_ref[0, 0]

    def block(px):
        start = FRONT - delay + px * 128
        total = wide[0, pl.ds(start, 128), :]
        for k in range(1, 4):
            total = total + wide[k, pl.ds(start - k, 128), :]
        return total

    def px_copy(i):
        px = xs[NX - i]
        return remote(part_b.at[i], part_in.at[i], PX_S, PX_R, at(px, z, b))

    for i in (2, 1, 3):
        part_b[i] = block(xs[NX - i]).astype(BF16)
        px_copy(i).start()
    acc = block(x)
    settle(part_in.at[1:NX], PX_R)
    for i in (1, 3, 2):
        acc = acc + part_in[i].astype(F32)
    line[...] = acc

    def pz_copy(i):
        pz = zs[NZ - AWAY[i]]
        return remote(line.at[pl.ds(pl.multiple_of(pz * 8, 8), 8)], line_in.at[i], PZ_S, PZ_R,
                      at(x, pz, b))

    for i in range(NZ - 1, 0, -1):
        pz_copy(i).start()

    settle(ex_in.at[1:NX * NB], EX_S)
    settle(base_in.at[1:NX], BASE_S)
    settle(msg.at[1:NZ], Z_S)
    for g in range(3):
        settle(pieces(g, 7), O_S + g)
    settle(part_in.at[1:NX], PX_S)
    settle(line_in.at[1:NZ], PZ_S)

    acc = line[pl.ds(pl.multiple_of(z * 8, 8), 8), :]
    settle(line_in.at[1:NZ], PZ_R)
    for i in range(1, NZ):
        acc = acc + line_in[i]
    out_ref[...] = acc


def body(donor, donor_elem, local_coords, owner, weights, offsets):
    hbm = pl.BlockSpec(memory_space=pltpu.HBM)
    dma = pltpu.SemaphoreType.DMA
    return pl.pallas_call(
        kernel,
        out_shape=jax.ShapeDtypeStruct((8, 128), F32),
        in_specs=[hbm] * 5 + [pl.BlockSpec(memory_space=pltpu.SMEM)],
        out_specs=pl.BlockSpec(memory_space=pltpu.VMEM),
        scratch_shapes=[
            pltpu.VMEM((4000, 128), BF16),
            pltpu.VMEM((1, 1024), I32),
            pltpu.VMEM((3, 1024), F32),
            pltpu.VMEM((64, 128), I32),
            pltpu.VMEM((2048, 128), BF16),
            pltpu.VMEM((128, 1024), BF16),
            pltpu.VMEM((128, 1024), BF16),
            pltpu.VMEM((1000, 1024), F32),
            pltpu.VMEM((128, 1024), BF16),
            pltpu.VMEM((8, 32, 128), F32),
            pltpu.VMEM((2048, 128), F32),
            pltpu.VMEM((512, 512), BF16),
            pltpu.VMEM((256, 128), BF16),
            pltpu.VMEM((512, 128), BF16),
            pltpu.VMEM((NX, 64, 128), BF16),
            pltpu.VMEM((NX * NB, 16, 128), BF16),
            pltpu.VMEM((NZ, 16, 128), BF16),
            pltpu.VMEM((NB, 256, 128), BF16),
            pltpu.VMEM((4, FRONT + TW, 128), F32),
            pltpu.VMEM((NX, 128, 128), BF16),
            pltpu.VMEM((NX, 128, 128), BF16),
            pltpu.VMEM((128, 128), F32),
            pltpu.VMEM((NZ, 8, 128), F32),
            dma((OWN + 6,)),
        ],
        compiler_params=pltpu.CompilerParams(
            collective_id=0, has_side_effects=True, vmem_limit_bytes=55228 * 1024),
    )(
        donor.reshape(4000, 128),
        donor_elem.reshape(1, 1024),
        local_coords,
        owner.reshape(64, 128),
        weights.reshape(2048, 128),
        offsets,
    )


def solution(mesh):
    return jax.shard_map(
        body,
        mesh=mesh,
        in_specs=(
            P("panel", None, None, "obs"),
            P("obs"),
            P(None, "obs"),
            P(),
            P("obs", None, None, "panel"),
            P("obs", "panel"),
        ),
        out_specs=P("panel", "obs"),
        check_vma=False,
    )
```

```python
import jax
import jax.numpy as jnp
from jax import lax
from jax.experimental import pallas as pl
from jax.experimental.pallas import tpu as pltpu
from jax.sharding import PartitionSpec as P

F32 = jnp.float32
BF16 = jnp.bfloat16
I32 = jnp.int32
SPOTS = (-1.0, -0.5, 0.0, 0.5, 1.0)
NX = 4
NZ = 16
NB = 8
FRONT = 264
TW = 512
NT = (((1,), (1,)), ((), ()))
NN = (((1,), (0,)), ((), ()))
MESH = pl.DeviceIdType.MESH
GROUPS = ((0, 80), (80, 96), (176, 80))
GROUP_ENDS = (5, 11, 16)
AWAY = (0, 1, 15, 2, 14, 3, 13, 4, 12, 5, 11, 6, 10, 7, 9, 8)
Z_FAR = AWAY[:0:-1]
OBS_FAR = (5, 4, 3, 7, 2, 6, 1, 0)
BACK = (0, 1, 6, 7, 4, 5, 2, 3)
BASE_S, BASE_R, EX_S, EX_R, Z_S, Z_R, Y_R, O_S, O_R, PX_S, PX_R, PZ_S, PZ_R, OWN = (
    0, 1, 2, 3, 4, 5, 8, 10, 13, 16, 17, 18, 19, 20)


def iota(shape, axis):
    return lax.broadcasted_iota(I32, shape, axis)


def dot(a, b, dims):
    return lax.dot_general(a, b, dims, preferred_element_type=F32)


def hit(cond):
    return jnp.where(cond, 1.0, 0.0).astype(BF16)


def flat_row(tiles):
    return jnp.concatenate([tiles[t:t + 1] for t in range(8)], axis=1)


def mix_pair(a, b, low):
    return jnp.where(low, a, pltpu.roll(b, 4, 0)), jnp.where(low, pltpu.roll(a, 4, 0), b)


def fill_table(coord_ref, table, greet):
    def table_step(tile):
        lanes = pl.ds(pl.multiple_of(tile * 128, 128), 128)
        factors = []
        for direction in range(3):
            x = jnp.broadcast_to(coord_ref[direction:direction + 1, lanes], (8, 128))
            column = []
            for one in range(5):
                value = None
                for two in range(5):
                    if two != one:
                        term = (x - SPOTS[two]) * (1.0 / (SPOTS[one] - SPOTS[two]))
                        value = term if value is None else value * term
                column.append(value)
            factors.append(column)
        low = iota((8, 128), 0) < 4
        pairs = [[fa * fb for fb in factors[1]] for fa in factors[0]]
        nodes = [pairs[n // 25][(n // 5) % 5] * factors[2][n % 5] for n in range(125)]
        for j in range(125):
            table[8 * j:8 * j + 8, lanes] = jnp.where(low, nodes[(2 * j) % 125], nodes[(2 * j + 1) % 125])

    def table_loop(tile, carry):
        for k in range(4):
            greet(4 * tile + k)
        table_step(tile)
        return carry

    lax.fori_loop(1, 8, table_loop, 0)
    for k in range(1, 4):
        greet(k)
    table_step(0)


def fill_sources(donor, hot, table, src, ready):
    edges = (0, 62, 63, 125, 187, 188, 250)
    for part in range(2):
        ready(part)
        sums = [None] * 6
        for piece in range(5):
            row = part * 2000 + piece * 400
            picked = dot(donor[row:row + 400, :], hot[...], NN)
            for k in range(6):
                begin, end = max(edges[k], piece * 50), min(edges[k + 1], piece * 50 + 50)
                if begin < end:
                    at = 8 * (begin - piece * 50)
                    size = 8 * (end - begin)
                    prod = picked[at:at + size] * table[8 * (begin % 125):8 * (begin % 125) + size, :]
                    value = jnp.sum(prod.reshape(end - begin, 8, 1024), axis=0)
                    sums[k] = value if sums[k] is None else sums[k] + value
        for half in range(2):
            first, mid, last = sums[3 * half:3 * half + 3]
            step = 16 * part + 2 * half
            even = first[:4] + first[4:] + mid[:4]
            odd = last[:4] + last[4:] + mid[4:]
            for tile in range(8):
                cols = slice(tile * 128, tile * 128 + 128)
                src[tile, pl.ds(step, 4, stride=4), :] = even[:, cols]
                src[tile, pl.ds(step + 1, 4, stride=4), :] = odd[:, cols]


def rank_points(own):
    member = iota((64, 1024), 0) == own
    member_f = jnp.where(member, 1.0, 0.0)
    member_b = member_f.astype(BF16)
    upper = hit(iota((128, 128), 0) < iota((128, 128), 1))
    ones = jnp.ones((128, 128), BF16)
    carry = jnp.zeros((64, 128), F32)
    ranks = []
    for tile in range(8):
        cols = slice(tile * 128, tile * 128 + 128)
        below = dot(member_b[:, cols], upper, NN) + carry
        ranks.append(jnp.sum(member_f[:, cols] * below, axis=0, keepdims=True))
        carry = carry + dot(member_b[:, cols], ones, NN)
    return jnp.concatenate(ranks, axis=1).astype(I32)


def fill_places(own, rank, place_base, place_extra):
    spot = jnp.where(rank < 12, (own & 7) * 16 + rank, -1)
    place_base[...] = hit(iota((128, 1024), 0) == spot)
    spot = jnp.where(rank >= 12, ((own >> 4) & 1) * 64 + (own & 15) * 4 + (rank & 3), -1)
    place_extra[...] = hit(iota((128, 1024), 0) == spot)


def group_base(sources, own, place, base_ref):
    group = own >> 3
    left = jnp.concatenate([jnp.where(group == g, sources, 0.0).astype(BF16) for g in range(8)], axis=0)
    grouped = dot(left, place[...], NT)
    row = iota((32, 128), 0)
    lane = iota((32, 128), 1)
    for g in range(8):
        x = grouped[g * 32:g * 32 + 32]
        for k in range(3):
            r, l = 4 << k, 16 << k
            rbit, lbit = (row >> (2 + k)) & 1, (lane >> (4 + k)) & 1
            up = pltpu.roll(pltpu.roll(x, 32 - r, 0), l, 1)
            down = pltpu.roll(pltpu.roll(x, r, 0), 128 - l, 1)
            x = jnp.where(rbit == lbit, x, jnp.where(rbit == 0, up, down))
        base_ref[g * 32:g * 32 + 32, :] = x.astype(BF16)


def group_extra(sources, own, rank, place, ex_ref):
    group = (own >> 5) * 8 + ((rank - 12) >> 2)
    half = iota((16, 128), 1) < 64
    for g in range(2):
        left = jnp.concatenate(
            [jnp.where(group == g * 8 + h, sources, 0.0).astype(BF16) for h in range(8)], axis=0)
        more = dot(left, place[...], NT)
        for h in range(8):
            r0, r1 = more[h * 32:h * 32 + 16], more[h * 32 + 16:h * 32 + 32]
            even = jnp.where(half, r0, pltpu.roll(r1, 64, 1))
            odd = jnp.where(half, pltpu.roll(r0, 64, 1), r1)
            at = ((2 * g) * 8 + h) * 16
            ex_ref[at:at + 16, :] = even.astype(BF16)
            at = ((2 * g + 1) * 8 + h) * 16
            ex_ref[at:at + 16, :] = odd.astype(BF16)


def order_weights(w_ref, owner_ref, panel, wf, w2_ref):
    wf[...] = w_ref[...].astype(F32)
    same = jnp.where(owner_ref[...] == panel, 1.0, 0.0)
    heavy = jnp.zeros((1, 1), F32)
    for block in range(1, 8):
        count = jnp.sum(jnp.sum(same[block * 8:block * 8 + 8], axis=0, keepdims=True), axis=1, keepdims=True)
        heavy = heavy + jnp.where(count > 28.0, float(block), 0.0)
    heavy = heavy.astype(I32)
    slot_lane = iota((1, 512), 1)
    relay, quant, slot = slot_lane >> 6, (slot_lane >> 4) & 3, slot_lane & 15
    panel_at = jnp.where(slot < 12, 12 * relay + jnp.where(relay > heavy, 32, 0) + slot,
                         12 * heavy + 4 * relay + slot)
    mover = hit(iota((512, 512), 0) == quant * 128 + panel_at)
    for k in range(4):
        rows = jnp.concatenate([wf[pl.ds(k * 4 + q, 128, stride=16), :].astype(BF16) for q in range(4)], axis=1)
        w2_ref[k * 128:k * 128 + 128, :] = dot(rows, mover, NN).astype(BF16)


def fill_messages(x, base_in, ex_in, msg):
    low = iota((8, 128), 0) < 4
    lane = iota((8, 128), 1)
    sums = []
    for px in range(NX):
        first = lax.rem(px + NX - x, NX) * NB
        total = ex_in[first].astype(F32)
        for pb in range(1, NB):
            total = total + ex_in[first + pb].astype(F32)
        sums.append(total)
    quants = []
    for v in range(2):
        rows = slice(v * 8, v * 8 + 8)
        e01, o01 = mix_pair(sums[0][rows], sums[1][rows], low)
        e23, o23 = mix_pair(sums[2][rows], sums[3][rows], low)
        quants += [(e01, e23), (o01, o23)]
    bases = [base_in[lax.rem(px + NX - x, NX)].astype(F32) for px in range(NX)]
    masks = [((lane & 63) >= 16 * q + 12) & ((lane & 63) < 16 * q + 16) for q in range(4)]
    for v in range(8):
        rows = slice(v * 8, v * 8 + 8)
        e01, o01 = mix_pair(bases[0][rows], bases[1][rows], low)
        e23, o23 = mix_pair(bases[2][rows], bases[3][rows], low)
        for pz, halves in ((2 * v, (e01, e23)), (2 * v + 1, (o01, o23))):
            done = []
            for h in range(2):
                value = halves[h]
                for q in range(4):
                    shift = (16 * q + 12 - 4 * pz) % 128
                    value = jnp.where(masks[q], pltpu.roll(quants[q][h], shift, 1), value)
                done.append(value)
            msg[pz] = jnp.concatenate(done, axis=0).astype(BF16)


def kernel(donor_hbm, elem_hbm, coord_hbm, owner_hbm, w_hbm, off_ref, out_ref,
           donor, elem_ref, coord_ref, owner_ref, weights, place_base, place_extra, table, hot, src, wf, w2, base_out, ex_out,
           base_in, ex_in, msg, held, wide, part_b, part_in, line, line_in,
           sems):
    panel = lax.axis_index("panel")
    b = lax.axis_index("obs")
    x = lax.div(panel, NZ)
    z = lax.rem(panel, NZ)
    y = lax.div(b, 2)
    core = lax.rem(b, 2)
    xs = [lax.rem(x + i, NX) for i in range(NX)]
    zs = [lax.rem(z + i, NZ) for i in range(NZ)]
    bs = [lax.rem(y + i // 2, 4) * 2 + (core if i % 2 == 0 else 1 - core) for i in range(NB)]

    def at(px, pz, pb):
        return {"panel": px * NZ + pz, "obs": pb}

    def remote(src_ref, dst_ref, send, recv, device):
        return pltpu.make_async_remote_copy(
            src_ref=src_ref, dst_ref=dst_ref, send_sem=sems.at[send], recv_sem=sems.at[recv],
            device_id=device, device_id_type=MESH)

    def settle(ref, which):
        pltpu.make_async_copy(ref, ref, sems.at[which]).wait()

    loads = [
        pltpu.make_async_copy(source, target, sems.at[OWN + i])
        for i, (source, target) in enumerate((
            (coord_hbm, coord_ref), (elem_hbm, elem_ref), (owner_hbm, owner_ref),
            (donor_hbm.at[0:2000], donor.at[0:2000]), (donor_hbm.at[2000:4000], donor.at[2000:4000]),
            (w_hbm, weights)))
    ]
    for load in loads:
        load.start()
    barrier = pltpu.get_barrier_semaphore()

    def greet(i):
        slot = lax.rem(x * NB + b + i, NX * NB)
        pl.semaphore_signal(barrier, inc=1, device_id=at(lax.div(slot, NB), z, lax.rem(slot, NB)),
                            device_id_type=MESH)

    for i in Z_FAR:
        pl.semaphore_signal(barrier, inc=1, device_id=at(x, zs[i], b), device_id_type=MESH)
    loads[0].wait()
    fill_table(coord_ref, table, greet)
    loads[1].wait()
    loads[2].wait()
    hot[...] = hit(iota((128, 1024), 0) == elem_ref[...] - b * 128)
    own = flat_row(owner_ref[pl.ds(pl.multiple_of(b * 8, 8), 8), :])
    rank = rank_points(own)
    fill_places(own, rank, place_base, place_extra)
    fill_sources(donor, hot, table, src, lambda part: loads[3 + part].wait())
    sources = jnp.concatenate([src[tile] for tile in range(8)], axis=1).astype(BF16).astype(F32)
    group_extra(sources, own, rank, place_extra, ex_out)
    pl.semaphore_wait(barrier, 46)

    def ex_copy(i, j):
        px, pb = xs[i], bs[j]
        back = ((NX - i) % NX) * NB + BACK[j]
        return remote(ex_out.at[pl.ds(pl.multiple_of((px * NB + pb) * 16, 16), 16)], ex_in.at[back],
                      EX_S, EX_R, at(px, z, pb))

    def base_copy(i):
        back = (NX - i) % NX
        return remote(base_out.at[pl.ds(pl.multiple_of(xs[i] * 64, 64), 64)], base_in.at[back],
                      BASE_S, BASE_R, at(xs[i], z, b))

    around = [(i, j) for i in (2, 1, 3, 0) for j in OBS_FAR if i or j]
    for i, j in around:
        ex_copy(i, j).start()
    group_base(sources, own, place_base, base_out)
    for i in (2, 1, 3):
        base_copy(i).start()
    own_base = pltpu.make_async_copy(base_out.at[pl.ds(pl.multiple_of(x * 64, 64), 64)], base_in.at[0], sems.at[OWN])
    own_ex = pltpu.make_async_copy(ex_out.at[pl.ds(pl.multiple_of((x * NB + b) * 16, 16), 16)], ex_in.at[0],
                                   sems.at[OWN + 1])
    own_base.start()
    own_ex.start()
    loads[5].wait()
    wide[:, 0:FRONT, :] = jnp.zeros((4, FRONT, 128), F32)
    order_weights(weights, owner_ref, panel, wf, w2)
    own_base.wait()
    own_ex.wait()
    settle(ex_in.at[1:NX * NB], EX_R)
    settle(base_in.at[1:NX], BASE_R)
    fill_messages(x, base_in, ex_in, msg)

    def z_copy(i):
        pz = zs[NZ - AWAY[i]]
        group = sum(i >= end for end in GROUP_ENDS)
        return remote(msg.at[pz], held.at[b, pl.ds(i * 16, 16)], Z_S, Z_R + group, at(x, pz, b))

    for i in range(NZ - 1, 0, -1):
        z_copy(i).start()
    own_z = pltpu.make_async_copy(msg.at[z], held.at[b, pl.ds(0, 16)], sems.at[OWN])
    own_z.start()
    own_z.wait()

    def o_copy(g, source, j, recv):
        rows = pl.ds(*GROUPS[g])
        return remote(held.at[source, rows], held.at[source, rows], O_S + g, recv, at(x, z, bs[j]))

    def pieces(g, n):
        return held.at[0:n, pl.ds(*GROUPS[g])]

    for g in range(3):
        first, size = GROUPS[g]
        skip = 16 if g == 0 else 0
        settle(held.at[b, pl.ds(first + skip, size - skip)], Z_R + g)
        for j in ((4, 2, 6, 1) if g < 2 else (5, 4, 3, 7, 2, 6, 1)):
            o_copy(g, b, j, Y_R + g if g < 2 and j > 1 else O_R + g).start()
    for g in range(2):
        settle(pieces(g, 3), Y_R + g)
        for j in (2, 6, 4):
            o_copy(g, bs[j], 1, O_R + g).start()
    for g in range(3):
        settle(pieces(g, 4 if g < 2 else 7), O_R + g)

    low_wide = iota((8, 512), 0) < 4
    halves = []
    for side in range(2):
        cols = slice(side * 64, side * 64 + 64)
        left = jnp.concatenate([held[pb][:, cols] for pb in range(NB)], axis=1)
        halves.append(dot(left, w2[...], NT))
    for i in range(NZ):
        time = FRONT + 8 * zs[AWAY[i]]
        for xp in range(2):
            rows = slice(i * 16 + xp * 8, i * 16 + xp * 8 + 8)
            pair = mix_pair(halves[0][rows], halves[1][rows], low_wide)
            for side in range(2):
                start = pl.multiple_of(time + 128 * (2 * xp + side), 8)
                for k in range(4):
                    wide[k, pl.ds(start, 8), :] = pair[side][:, k * 128:k * 128 + 128]
    delay = off_ref[0, 0]

    def block(px):
        start = FRONT - delay + px * 128
        total = wide[0, pl.ds(start, 128), :]
        for k in range(1, 4):
            total = total + wide[k, pl.ds(start - k, 128), :]
        return total

    def px_copy(i):
        px = xs[NX - i]
        return remote(part_b.at[i], part_in.at[i], PX_S, PX_R, at(px, z, b))

    for i in (2, 1, 3):
        part_b[i] = block(xs[NX - i]).astype(BF16)
        px_copy(i).start()
    acc = block(x)
    settle(part_in.at[1:NX], PX_R)
    for i in (1, 3, 2):
        acc = acc + part_in[i].astype(F32)
    line[...] = acc

    def pz_copy(i):
        pz = zs[NZ - AWAY[i]]
        return remote(line.at[pl.ds(pl.multiple_of(pz * 8, 8), 8)], line_in.at[i], PZ_S, PZ_R,
                      at(x, pz, b))

    for i in range(NZ - 1, 0, -1):
        pz_copy(i).start()

    settle(ex_in.at[1:NX * NB], EX_S)
    settle(base_in.at[1:NX], BASE_S)
    settle(msg.at[1:NZ], Z_S)
    for g in range(3):
        settle(pieces(g, 7), O_S + g)
    settle(part_in.at[1:NX], PX_S)
    settle(line_in.at[1:NZ], PZ_S)

    acc = line[pl.ds(pl.multiple_of(z * 8, 8), 8), :]
    settle(line_in.at[1:NZ], PZ_R)
    for i in range(1, NZ):
        acc = acc + line_in[i]
    out_ref[...] = acc


def body(donor, donor_elem, local_coords, owner, weights, offsets):
    hbm = pl.BlockSpec(memory_space=pltpu.HBM)
    dma = pltpu.SemaphoreType.DMA
    return pl.pallas_call(
        kernel,
        out_shape=jax.ShapeDtypeStruct((8, 128), F32),
        in_specs=[hbm] * 5 + [pl.BlockSpec(memory_space=pltpu.SMEM)],
        out_specs=pl.BlockSpec(memory_space=pltpu.VMEM),
        scratch_shapes=[
            pltpu.VMEM((4000, 128), BF16),
            pltpu.VMEM((1, 1024), I32),
            pltpu.VMEM((3, 1024), F32),
            pltpu.VMEM((64, 128), I32),
            pltpu.VMEM((2048, 128), BF16),
            pltpu.VMEM((128, 1024), BF16),
            pltpu.VMEM((128, 1024), BF16),
            pltpu.VMEM((1000, 1024), F32),
            pltpu.VMEM((128, 1024), BF16),
            pltpu.VMEM((8, 32, 128), F32),
            pltpu.VMEM((2048, 128), F32),
            pltpu.VMEM((512, 512), BF16),
            pltpu.VMEM((256, 128), BF16),
            pltpu.VMEM((512, 128), BF16),
            pltpu.VMEM((NX, 64, 128), BF16),
            pltpu.VMEM((NX * NB, 16, 128), BF16),
            pltpu.VMEM((NZ, 16, 128), BF16),
            pltpu.VMEM((NB, 256, 128), BF16),
            pltpu.VMEM((4, FRONT + TW, 128), F32),
            pltpu.VMEM((NX, 128, 128), BF16),
            pltpu.VMEM((NX, 128, 128), BF16),
            pltpu.VMEM((128, 128), F32),
            pltpu.VMEM((NZ, 8, 128), F32),
            dma((OWN + 6,)),
        ],
        compiler_params=pltpu.CompilerParams(
            collective_id=0, has_side_effects=True, vmem_limit_bytes=55228 * 1024),
    )(
        donor.reshape(4000, 128),
        donor_elem.reshape(1, 1024),
        local_coords,
        owner.reshape(64, 128),
        weights.reshape(2048, 128),
        offsets,
    )


def solution(mesh):
    return jax.shard_map(
        body,
        mesh=mesh,
        in_specs=(
            P("panel", None, None, "obs"),
            P("obs"),
            P(None, "obs"),
            P(),
            P("obs", None, None, "panel"),
            P("obs", "panel"),
        ),
        out_specs=P("panel", "obs"),
        check_vma=False,
    )
```

```python
import jax
import jax.numpy as jnp
from jax import lax
from jax.experimental import pallas as pl
from jax.experimental.pallas import tpu as pltpu
from jax.sharding import PartitionSpec as P

F32 = jnp.float32
BF16 = jnp.bfloat16
I32 = jnp.int32
SPOTS = (-1.0, -0.5, 0.0, 0.5, 1.0)
NX = 4
NZ = 16
NB = 8
FRONT = 264
TW = 512
NT = (((1,), (1,)), ((), ()))
NN = (((1,), (0,)), ((), ()))
MESH = pl.DeviceIdType.MESH
GROUPS = ((0, 80), (80, 96), (176, 80))
GROUP_ENDS = (5, 11, 16)
AWAY = (0, 1, 15, 2, 14, 3, 13, 4, 12, 5, 11, 6, 10, 7, 9, 8)
Z_FAR = AWAY[:0:-1]
OBS_FAR = (5, 4, 3, 7, 2, 6, 1, 0)
BACK = (0, 1, 6, 7, 4, 5, 2, 3)
BASE_S, BASE_R, EX_S, EX_R, Z_S, Z_R, Y_R, O_S, O_R, PX_S, PX_R, PZ_S, PZ_R, OWN = (
    0, 1, 2, 3, 4, 5, 8, 10, 13, 16, 17, 18, 19, 20)


def iota(shape, axis):
    return lax.broadcasted_iota(I32, shape, axis)


def dot(a, b, dims):
    return lax.dot_general(a, b, dims, preferred_element_type=F32)


def hit(cond):
    return jnp.where(cond, 1.0, 0.0).astype(BF16)


def flat_row(tiles):
    return jnp.concatenate([tiles[t:t + 1] for t in range(8)], axis=1)


def mix_pair(a, b, low):
    return jnp.where(low, a, pltpu.roll(b, 4, 0)), jnp.where(low, pltpu.roll(a, 4, 0), b)


def fill_table(coord_ref, table, greet):
    def table_step(tile):
        lanes = pl.ds(pl.multiple_of(tile * 128, 128), 128)
        factors = []
        for direction in range(3):
            x = jnp.broadcast_to(coord_ref[direction:direction + 1, lanes], (8, 128))
            column = []
            for one in range(5):
                value = None
                for two in range(5):
                    if two != one:
                        term = (x - SPOTS[two]) * (1.0 / (SPOTS[one] - SPOTS[two]))
                        value = term if value is None else value * term
                column.append(value)
            factors.append(column)
        low = iota((8, 128), 0) < 4
        pairs = [[fa * fb for fb in factors[1]] for fa in factors[0]]
        nodes = [pairs[n // 25][(n // 5) % 5] * factors[2][n % 5] for n in range(125)]
        for j in range(125):
            table[8 * j:8 * j + 8, lanes] = jnp.where(low, nodes[(2 * j) % 125], nodes[(2 * j + 1) % 125])

    def table_loop(tile, carry):
        for k in range(4):
            greet(4 * tile + k)
        table_step(tile)
        return carry

    lax.fori_loop(1, 8, table_loop, 0)
    for k in range(1, 4):
        greet(k)
    table_step(0)


def fill_sources(donor, hot, table, src, ready):
    edges = (0, 62, 63, 125, 187, 188, 250)
    for part in range(2):
        ready(part)
        sums = [None] * 6
        for piece in range(5):
            row = part * 2000 + piece * 400
            picked = dot(donor[row:row + 400, :], hot[...], NN)
            for k in range(6):
                begin, end = max(edges[k], piece * 50), min(edges[k + 1], piece * 50 + 50)
                if begin < end:
                    at = 8 * (begin - piece * 50)
                    size = 8 * (end - begin)
                    prod = picked[at:at + size] * table[8 * (begin % 125):8 * (begin % 125) + size, :]
                    value = jnp.sum(prod.reshape(end - begin, 8, 1024), axis=0)
                    sums[k] = value if sums[k] is None else sums[k] + value
        for half in range(2):
            first, mid, last = sums[3 * half:3 * half + 3]
            step = 16 * part + 2 * half
            even = first[:4] + first[4:] + mid[:4]
            odd = last[:4] + last[4:] + mid[4:]
            for tile in range(8):
                cols = slice(tile * 128, tile * 128 + 128)
                src[tile, pl.ds(step, 4, stride=4), :] = even[:, cols]
                src[tile, pl.ds(step + 1, 4, stride=4), :] = odd[:, cols]


def rank_points(own):
    member = iota((64, 1024), 0) == own
    member_f = jnp.where(member, 1.0, 0.0)
    member_b = member_f.astype(BF16)
    upper = hit(iota((128, 128), 0) < iota((128, 128), 1))
    ones = jnp.ones((128, 128), BF16)
    carry = jnp.zeros((64, 128), F32)
    ranks = []
    for tile in range(8):
        cols = slice(tile * 128, tile * 128 + 128)
        below = dot(member_b[:, cols], upper, NN) + carry
        ranks.append(jnp.sum(member_f[:, cols] * below, axis=0, keepdims=True))
        carry = carry + dot(member_b[:, cols], ones, NN)
    return jnp.concatenate(ranks, axis=1).astype(I32)


def fill_places(own, rank, place_base, place_extra):
    spot = jnp.where(rank < 12, (own & 7) * 16 + rank, -1)
    place_base[...] = hit(iota((128, 1024), 0) == spot)
    spot = jnp.where(rank >= 12, ((own >> 4) & 1) * 64 + (own & 15) * 4 + (rank & 3), -1)
    place_extra[...] = hit(iota((128, 1024), 0) == spot)


def group_base(sources, own, place, base_ref):
    group = own >> 3
    left = jnp.concatenate([jnp.where(group == g, sources, 0.0).astype(BF16) for g in range(8)], axis=0)
    grouped = dot(left, place[...], NT)
    row = iota((32, 128), 0)
    lane = iota((32, 128), 1)
    for g in range(8):
        x = grouped[g * 32:g * 32 + 32]
        for k in range(3):
            r, l = 4 << k, 16 << k
            rbit, lbit = (row >> (2 + k)) & 1, (lane >> (4 + k)) & 1
            up = pltpu.roll(pltpu.roll(x, 32 - r, 0), l, 1)
            down = pltpu.roll(pltpu.roll(x, r, 0), 128 - l, 1)
            x = jnp.where(rbit == lbit, x, jnp.where(rbit == 0, up, down))
        base_ref[g * 32:g * 32 + 32, :] = x.astype(BF16)


def group_extra(sources, own, rank, place, ex_ref):
    group = (own >> 5) * 8 + ((rank - 12) >> 2)
    half = iota((16, 128), 1) < 64
    for g in range(2):
        left = jnp.concatenate(
            [jnp.where(group == g * 8 + h, sources, 0.0).astype(BF16) for h in range(8)], axis=0)
        more = dot(left, place[...], NT)
        for h in range(8):
            r0, r1 = more[h * 32:h * 32 + 16], more[h * 32 + 16:h * 32 + 32]
            even = jnp.where(half, r0, pltpu.roll(r1, 64, 1))
            odd = jnp.where(half, pltpu.roll(r0, 64, 1), r1)
            at = ((2 * g) * 8 + h) * 16
            ex_ref[at:at + 16, :] = even.astype(BF16)
            at = ((2 * g + 1) * 8 + h) * 16
            ex_ref[at:at + 16, :] = odd.astype(BF16)


def order_weights(w_ref, owner_ref, panel, wf, w2_ref):
    wf[...] = w_ref[...].astype(F32)
    same = jnp.where(owner_ref[...] == panel, 1.0, 0.0)
    heavy = jnp.zeros((1, 1), F32)
    for block in range(1, 8):
        count = jnp.sum(jnp.sum(same[block * 8:block * 8 + 8], axis=0, keepdims=True), axis=1, keepdims=True)
        heavy = heavy + jnp.where(count > 28.0, float(block), 0.0)
    heavy = heavy.astype(I32)
    slot_lane = iota((1, 512), 1)
    relay, quant, slot = slot_lane >> 6, (slot_lane >> 4) & 3, slot_lane & 15
    panel_at = jnp.where(slot < 12, 12 * relay + jnp.where(relay > heavy, 32, 0) + slot,
                         12 * heavy + 4 * relay + slot)
    mover = hit(iota((512, 512), 0) == quant * 128 + panel_at)
    for k in range(4):
        rows = jnp.concatenate([wf[pl.ds(k * 4 + q, 128, stride=16), :].astype(BF16) for q in range(4)], axis=1)
        w2_ref[k * 128:k * 128 + 128, :] = dot(rows, mover, NN).astype(BF16)


def fill_messages(x, base_in, ex_in, msg):
    low = iota((8, 128), 0) < 4
    lane = iota((8, 128), 1)
    sums = []
    for px in range(NX):
        first = lax.rem(px + NX - x, NX) * NB
        total = ex_in[first].astype(F32)
        for pb in range(1, NB):
            total = total + ex_in[first + pb].astype(F32)
        sums.append(total)
    quants = []
    for v in range(2):
        rows = slice(v * 8, v * 8 + 8)
        e01, o01 = mix_pair(sums[0][rows], sums[1][rows], low)
        e23, o23 = mix_pair(sums[2][rows], sums[3][rows], low)
        quants += [(e01, e23), (o01, o23)]
    bases = [base_in[lax.rem(px + NX - x, NX)].astype(F32) for px in range(NX)]
    masks = [((lane & 63) >= 16 * q + 12) & ((lane & 63) < 16 * q + 16) for q in range(4)]
    for v in range(8):
        rows = slice(v * 8, v * 8 + 8)
        e01, o01 = mix_pair(bases[0][rows], bases[1][rows], low)
        e23, o23 = mix_pair(bases[2][rows], bases[3][rows], low)
        for pz, halves in ((2 * v, (e01, e23)), (2 * v + 1, (o01, o23))):
            done = []
            for h in range(2):
                value = halves[h]
                for q in range(4):
                    shift = (16 * q + 12 - 4 * pz) % 128
                    value = jnp.where(masks[q], pltpu.roll(quants[q][h], shift, 1), value)
                done.append(value)
            msg[pz] = jnp.concatenate(done, axis=0).astype(BF16)


def kernel(donor_hbm, elem_hbm, coord_hbm, owner_hbm, w_hbm, off_ref, out_ref,
           donor, elem_ref, coord_ref, owner_ref, weights, place_base, place_extra, table, hot, src, wf, w2, base_out, ex_out,
           base_in, ex_in, msg, held, wide, part_b, part_in, line, line_in,
           sems):
    panel = lax.axis_index("panel")
    b = lax.axis_index("obs")
    x = lax.div(panel, NZ)
    z = lax.rem(panel, NZ)
    y = lax.div(b, 2)
    core = lax.rem(b, 2)
    xs = [lax.rem(x + i, NX) for i in range(NX)]
    zs = [lax.rem(z + i, NZ) for i in range(NZ)]
    bs = [lax.rem(y + i // 2, 4) * 2 + (core if i % 2 == 0 else 1 - core) for i in range(NB)]

    def at(px, pz, pb):
        return {"panel": px * NZ + pz, "obs": pb}

    def remote(src_ref, dst_ref, send, recv, device):
        return pltpu.make_async_remote_copy(
            src_ref=src_ref, dst_ref=dst_ref, send_sem=sems.at[send], recv_sem=sems.at[recv],
            device_id=device, device_id_type=MESH)

    def settle(ref, which):
        pltpu.make_async_copy(ref, ref, sems.at[which]).wait()

    loads = [
        pltpu.make_async_copy(source, target, sems.at[OWN + i])
        for i, (source, target) in enumerate((
            (coord_hbm, coord_ref), (elem_hbm, elem_ref), (owner_hbm, owner_ref),
            (donor_hbm.at[0:2000], donor.at[0:2000]), (donor_hbm.at[2000:4000], donor.at[2000:4000]),
            (w_hbm, weights)))
    ]
    for load in loads:
        load.start()
    barrier = pltpu.get_barrier_semaphore()

    def greet(i):
        slot = lax.rem(x * NB + b + i, NX * NB)
        pl.semaphore_signal(barrier, inc=1, device_id=at(lax.div(slot, NB), z, lax.rem(slot, NB)),
                            device_id_type=MESH)

    for i in Z_FAR:
        pl.semaphore_signal(barrier, inc=1, device_id=at(x, zs[i], b), device_id_type=MESH)
    loads[0].wait()
    fill_table(coord_ref, table, greet)
    loads[1].wait()
    loads[2].wait()
    hot[...] = hit(iota((128, 1024), 0) == elem_ref[...] - b * 128)
    own = flat_row(owner_ref[pl.ds(pl.multiple_of(b * 8, 8), 8), :])
    rank = rank_points(own)
    fill_places(own, rank, place_base, place_extra)
    fill_sources(donor, hot, table, src, lambda part: loads[3 + part].wait())
    sources = jnp.concatenate([src[tile] for tile in range(8)], axis=1).astype(BF16).astype(F32)
    group_extra(sources, own, rank, place_extra, ex_out)
    pl.semaphore_wait(barrier, 46)

    def ex_copy(i, j):
        px, pb = xs[i], bs[j]
        back = ((NX - i) % NX) * NB + BACK[j]
        return remote(ex_out.at[pl.ds(pl.multiple_of((px * NB + pb) * 16, 16), 16)], ex_in.at[back],
                      EX_S, EX_R, at(px, z, pb))

    def base_copy(i):
        back = (NX - i) % NX
        return remote(base_out.at[pl.ds(pl.multiple_of(xs[i] * 64, 64), 64)], base_in.at[back],
                      BASE_S, BASE_R, at(xs[i], z, b))

    around = [(i, j) for i in (2, 1, 3, 0) for j in OBS_FAR if i or j]
    for i, j in around:
        ex_copy(i, j).start()
    group_base(sources, own, place_base, base_out)
    for i in (2, 1, 3):
        base_copy(i).start()
    own_base = pltpu.make_async_copy(base_out.at[pl.ds(pl.multiple_of(x * 64, 64), 64)], base_in.at[0], sems.at[OWN])
    own_ex = pltpu.make_async_copy(ex_out.at[pl.ds(pl.multiple_of((x * NB + b) * 16, 16), 16)], ex_in.at[0],
                                   sems.at[OWN + 1])
    own_base.start()
    own_ex.start()
    loads[5].wait()
    wide[:, 0:FRONT, :] = jnp.zeros((4, FRONT, 128), F32)
    order_weights(weights, owner_ref, panel, wf, w2)
    own_base.wait()
    own_ex.wait()
    settle(ex_in.at[1:NX * NB], EX_R)
    settle(base_in.at[1:NX], BASE_R)
    fill_messages(x, base_in, ex_in, msg)

    def z_copy(i):
        pz = zs[NZ - AWAY[i]]
        group = sum(i >= end for end in GROUP_ENDS)
        return remote(msg.at[pz], held.at[b, pl.ds(i * 16, 16)], Z_S, Z_R + group, at(x, pz, b))

    for i in range(NZ - 1, 0, -1):
        z_copy(i).start()
    own_z = pltpu.make_async_copy(msg.at[z], held.at[b, pl.ds(0, 16)], sems.at[OWN])
    own_z.start()
    own_z.wait()

    def o_copy(g, source, j, recv):
        rows = pl.ds(*GROUPS[g])
        return remote(held.at[source, rows], held.at[source, rows], O_S + g, recv, at(x, z, bs[j]))

    def pieces(g, n):
        return held.at[0:n, pl.ds(*GROUPS[g])]

    def pass_on(g):
        settle(pieces(g, 3), Y_R + g)
        for j in (2, 6, 4):
            o_copy(g, bs[j], 1, O_R + g).start()

    for g in range(3):
        if g == 2:
            pass_on(0)
        first, size = GROUPS[g]
        skip = 16 if g == 0 else 0
        settle(held.at[b, pl.ds(first + skip, size - skip)], Z_R + g)
        for j in ((4, 2, 6, 1) if g < 2 else (5, 4, 3, 7, 2, 6, 1)):
            o_copy(g, b, j, Y_R + g if g < 2 and j > 1 else O_R + g).start()
    pass_on(1)
    for g in range(3):
        settle(pieces(g, 4 if g < 2 else 7), O_R + g)

    low_wide = iota((8, 512), 0) < 4
    halves = []
    for side in range(2):
        cols = slice(side * 64, side * 64 + 64)
        left = jnp.concatenate([held[pb][:, cols] for pb in range(NB)], axis=1)
        halves.append(dot(left, w2[...], NT))
    for i in range(NZ):
        time = FRONT + 8 * zs[AWAY[i]]
        for xp in range(2):
            rows = slice(i * 16 + xp * 8, i * 16 + xp * 8 + 8)
            pair = mix_pair(halves[0][rows], halves[1][rows], low_wide)
            for side in range(2):
                start = pl.multiple_of(time + 128 * (2 * xp + side), 8)
                for k in range(4):
                    wide[k, pl.ds(start, 8), :] = pair[side][:, k * 128:k * 128 + 128]
    delay = off_ref[0, 0]

    def block(px):
        start = FRONT - delay + px * 128
        total = wide[0, pl.ds(start, 128), :]
        for k in range(1, 4):
            total = total + wide[k, pl.ds(start - k, 128), :]
        return total

    def px_copy(i):
        px = xs[NX - i]
        return remote(part_b.at[i], part_in.at[i], PX_S, PX_R, at(px, z, b))

    for i in (2, 1, 3):
        part_b[i] = block(xs[NX - i]).astype(BF16)
        px_copy(i).start()
    acc = block(x)
    settle(part_in.at[1:NX], PX_R)
    for i in (1, 3, 2):
        acc = acc + part_in[i].astype(F32)
    line[...] = acc

    def pz_copy(i):
        pz = zs[NZ - AWAY[i]]
        return remote(line.at[pl.ds(pl.multiple_of(pz * 8, 8), 8)], line_in.at[i], PZ_S, PZ_R,
                      at(x, pz, b))

    for i in range(NZ - 1, 0, -1):
        pz_copy(i).start()

    settle(ex_in.at[1:NX * NB], EX_S)
    settle(base_in.at[1:NX], BASE_S)
    settle(msg.at[1:NZ], Z_S)
    for g in range(3):
        settle(pieces(g, 7), O_S + g)
    settle(part_in.at[1:NX], PX_S)
    settle(line_in.at[1:NZ], PZ_S)

    acc = line[pl.ds(pl.multiple_of(z * 8, 8), 8), :]
    settle(line_in.at[1:NZ], PZ_R)
    for i in range(1, NZ):
        acc = acc + line_in[i]
    out_ref[...] = acc


def body(donor, donor_elem, local_coords, owner, weights, offsets):
    hbm = pl.BlockSpec(memory_space=pltpu.HBM)
    dma = pltpu.SemaphoreType.DMA
    return pl.pallas_call(
        kernel,
        out_shape=jax.ShapeDtypeStruct((8, 128), F32),
        in_specs=[hbm] * 5 + [pl.BlockSpec(memory_space=pltpu.SMEM)],
        out_specs=pl.BlockSpec(memory_space=pltpu.VMEM),
        scratch_shapes=[
            pltpu.VMEM((4000, 128), BF16),
            pltpu.VMEM((1, 1024), I32),
            pltpu.VMEM((3, 1024), F32),
            pltpu.VMEM((64, 128), I32),
            pltpu.VMEM((2048, 128), BF16),
            pltpu.VMEM((128, 1024), BF16),
            pltpu.VMEM((128, 1024), BF16),
            pltpu.VMEM((1000, 1024), F32),
            pltpu.VMEM((128, 1024), BF16),
            pltpu.VMEM((8, 32, 128), F32),
            pltpu.VMEM((2048, 128), F32),
            pltpu.VMEM((512, 512), BF16),
            pltpu.VMEM((256, 128), BF16),
            pltpu.VMEM((512, 128), BF16),
            pltpu.VMEM((NX, 64, 128), BF16),
            pltpu.VMEM((NX * NB, 16, 128), BF16),
            pltpu.VMEM((NZ, 16, 128), BF16),
            pltpu.VMEM((NB, 256, 128), BF16),
            pltpu.VMEM((4, FRONT + TW, 128), F32),
            pltpu.VMEM((NX, 128, 128), BF16),
            pltpu.VMEM((NX, 128, 128), BF16),
            pltpu.VMEM((128, 128), F32),
            pltpu.VMEM((NZ, 8, 128), F32),
            dma((OWN + 6,)),
        ],
        compiler_params=pltpu.CompilerParams(
            collective_id=0, has_side_effects=True, vmem_limit_bytes=55228 * 1024),
    )(
        donor.reshape(4000, 128),
        donor_elem.reshape(1, 1024),
        local_coords,
        owner.reshape(64, 128),
        weights.reshape(2048, 128),
        offsets,
    )


def solution(mesh):
    return jax.shard_map(
        body,
        mesh=mesh,
        in_specs=(
            P("panel", None, None, "obs"),
            P("obs"),
            P(None, "obs"),
            P(),
            P("obs", None, None, "panel"),
            P("obs", "panel"),
        ),
        out_specs=P("panel", "obs"),
        check_vma=False,
    )
```
